32 devices in a mesh: tm: 8 (over z, y), space: 4 (over x, core).
Axes of the slice: x: 2, y: 2, z: 4, core: 2. Of those that a mesh axis runs over, the one named last changes fastest.
Arguments:
- frames_in: bfloat16 [8, 256, 128, 128], P('tm', None, 'space'), may hold values from -6 to 6
- conv_weight: bfloat16 [3, 3, 256, 256], replicated, may hold values from -0.125 to 0.125
- out_weight: bfloat16 [256, 256], replicated, may hold values from -0.375 to 0.375
- skip_gain: float32 [256], replicated, may hold values from -4 to 4
- decays: float32 [8, 256], P('tm'), may hold values from 0.25 to 1, as said below
Outputs:
- frames_out: bfloat16 [8, 256, 128, 128], P('tm', None, 'space')
The draws below stay inside these ranges and needn't reach their ends.
Inputs may be any that keep to these rules, and one draw needn't show every extreme that they name: `decays`: every entry lies strictly below 1.
All inputs are finite; a program needn't handle non-finite values.
Results may differ from the reference program's by a relative error of at most 0.0041.
Values may be sent and summed in bfloat16 or wider, within the bound.
No kernel may reach another device: no remote copies, remote signals or barrier semaphores. Data moves between devices by JAX's collectives and lax.ppermute only.
A program may use at most 320 MiB of HBM per device.

```python
import math
import jax
import jax.numpy as jnp
from jax import lax

C = 256
P_SIZE = 256
H = 128
W = 128
SPAN_STEPS = 8


def draw_decays(key, part):
    seed_handles = jax.random.split(key, 6)
    slow_share = 0.5
    slow = jax.random.uniform(seed_handles[0], (P_SIZE,)) < slow_share
    rate_slow = jnp.exp(jax.random.uniform(seed_handles[1], (P_SIZE,), minval=math.log(0.3 / SPAN_STEPS), maxval=math.log(2.0 / SPAN_STEPS)))
    rate_fast = 1.0 / jax.random.uniform(seed_handles[2], (P_SIZE,), minval=10.0, maxval=17.0)
    base = jnp.where(slow, rate_slow, rate_fast)
    rough = jax.random.uniform(seed_handles[3], (SPAN_STEPS, P_SIZE), minval=0.5, maxval=2.0)
    kept = jnp.exp(-base[None, :] * rough)
    spike_instant = jax.random.randint(seed_handles[4], (4,), 0, SPAN_STEPS)
    impacted_steps = jnp.any(jnp.arange(SPAN_STEPS)[:, None] == spike_instant[None, :], axis=1)
    factor = jax.random.uniform(seed_handles[5], (SPAN_STEPS, P_SIZE), minval=0.5, maxval=0.8)
    return jnp.where(impacted_steps[:, None], kept * factor, kept).astype(jnp.float32)


def block_levels(rng, extent, cuts, smallest, largest):
    def one(axis_at, blocks):
        heights = jax.random.uniform(jax.random.fold_in(jax.random.fold_in(rng, 6), axis_at), (blocks,), jnp.float32, smallest / len(cuts), largest / len(cuts))
        return jnp.repeat(jnp.exp(heights), extent[axis_at] // blocks).reshape((-1,) + (1,) * (len(extent) - axis_at - 1))

    gain = one(*cuts[0])
    for cut in cuts[1:]:
        gain = gain * one(*cut)
    return gain


def noise(stream_key, extent, spread, bound, cuts=(), dtype=jnp.bfloat16):
    drawn = spread * jax.random.normal(stream_key, extent, jnp.float32)
    if cuts:
        drawn = drawn * block_levels(stream_key, extent, cuts, -0.22, 0.18)
    return jnp.clip(drawn, -bound, bound).astype(dtype)


def setup_inputs(seed: int = 0) -> dict:
    streams_of = jax.random.split(jax.random.key(seed), 6)
    return {
        "frames_in": noise(streams_of[0], (SPAN_STEPS, C, H, W), 1.0, 6.0, ((0, 8), (2, 4))),
        "conv_weight": noise(streams_of[1], (3, 3, P_SIZE, C), (9 * C) ** -0.5, 0.125),
        "out_weight": noise(streams_of[2], (C, P_SIZE), P_SIZE ** -0.5, 0.375),
        "skip_gain": noise(streams_of[3], (C,), 0.7, 4.0, (), jnp.float32),
        "decays": draw_decays(jax.random.fold_in(streams_of[5], 71), 0),
    }


def reference(frames_in, conv_weight, out_weight, skip_gain, decays):
    conv_f32 = conv_weight.astype(jnp.float32)
    out_f32 = out_weight.astype(jnp.float32)

    def frame_step(memory, frame_data):
        frame_x, frame_decay = frame_data
        frame_f32 = frame_x.astype(jnp.float32)
        padded = jnp.pad(frame_f32, ((0, 0), (1, 1), (1, 1)))
        driving = jnp.zeros((P_SIZE, H, W), jnp.float32)
        for vertical_shift in range(3):
            for col_off in range(3):
                driving = driving + jnp.einsum('pc,chw->phw', conv_f32[vertical_shift, col_off], padded[:, vertical_shift:vertical_shift + H, col_off:col_off + W])
        in_gain = jnp.sqrt(1.0 - frame_decay * frame_decay)
        memory = frame_decay[:, None, None] * memory + in_gain[:, None, None] * driving
        rounded = lax.optimization_barrier(memory.astype(jnp.bfloat16)).astype(jnp.float32)
        output = jnp.einsum('cp,phw->chw', out_f32, rounded) + skip_gain[:, None, None] * frame_f32
        return (memory, output.astype(jnp.bfloat16))
    start = jnp.zeros((P_SIZE, H, W), jnp.float32)
    ending, output_frames = lax.scan(frame_step, start, (frames_in, decays))
    return output_frames
```

```python
import functools

import jax
import jax.numpy as jnp
from jax import lax
from jax.experimental import pallas as pl
from jax.experimental.pallas import tpu as pltpu
from jax.sharding import PartitionSpec as P

CHUNK = 2
FIRST = 2
MIB = 1 << 20

VMEM = pl.BlockSpec(memory_space=pltpu.VMEM)
ANY = pl.BlockSpec(memory_space=pl.ANY)
SMEM = pl.BlockSpec(memory_space=pltpu.SMEM)


def params(mib):
    return pltpu.CompilerParams(vmem_limit_bytes=mib * MIB)


def conv_kernel(chunks, halo, place, rows_in, *refs):
    refs = list(refs)
    halo_ref = refs.pop(0) if halo else None
    weight, coefs = refs.pop(0), refs.pop(0)
    outs = refs[:chunks]
    rows, shifted, made, sems = refs[chunks:]
    total = rows.shape[0]
    copied = total - 1 if halo else total
    channels, width = rows.shape[1], rows.shape[2]
    main = pltpu.make_async_copy(
        rows_in.at[pl.ds(place[0], copied)], rows.at[pl.ds(place[1], copied)], sems.at[chunks]
    )
    main.start()
    main.wait()
    if halo:
        rows[place[4]] = halo_ref[...]
    lane = lax.broadcasted_iota(jnp.int32, (channels, width), 1)

    def shift(r, _):
        row = rows[r].astype(jnp.float32)
        left = jnp.where(lane == 0, 0.0, pltpu.roll(row, 1, 1))
        right = jnp.where(lane == width - 1, 0.0, pltpu.roll(row, width - 1, 1))
        shifted[r, :channels] = left.astype(jnp.bfloat16)
        shifted[r, channels : 2 * channels] = rows[r]
        shifted[r, 2 * channels :] = right.astype(jnp.bfloat16)
        return _

    lax.fori_loop(0, total, shift, 0, unroll=2)
    gain = coefs[:, 0:1]
    taps = jnp.concatenate([weight[i, j] for i in range(3) for j in range(3)], axis=1)

    def one(k, _):
        r = place[3] + k * place[2]
        window = jnp.concatenate(
            [
                jnp.concatenate([shifted[r + i + q] for q in range(CHUNK)], axis=1)
                for i in range(3)
            ],
            axis=0,
        )
        drive = gain * jnp.dot(taps, window, preferred_element_type=jnp.float32)
        for q in range(CHUNK):
            made[k, q] = drive[:, q * width : (q + 1) * width].astype(made.dtype)
        for n, out in enumerate(outs):

            @pl.when(k == n)
            def start():
                pltpu.make_async_copy(made.at[n], out, sems.at[n]).start()

        return _

    lax.fori_loop(0, chunks, one, 0)
    for n, out in enumerate(outs):
        pltpu.make_async_copy(made.at[n], out, sems.at[n]).wait()


def conv(rows_in, halo, weight, coefs, place, chunks, dtype):
    channels, width = rows_in.shape[1], rows_in.shape[2]
    states = weight.shape[2]
    total = chunks * CHUNK + 2
    shape = (CHUNK, states, width)
    outs = [jax.ShapeDtypeStruct(shape, dtype)] * chunks
    operands = [place, rows_in] + ([halo] if halo is not None else []) + [weight, coefs]
    specs = [SMEM, ANY] + ([VMEM] if halo is not None else []) + [VMEM, VMEM]
    return pl.pallas_call(
        functools.partial(conv_kernel, chunks, halo is not None),
        out_shape=outs,
        in_specs=specs,
        out_specs=[ANY] * chunks,
        scratch_shapes=[
            pltpu.VMEM((total, channels, width), rows_in.dtype),
            pltpu.VMEM((total, 3 * channels, width), rows_in.dtype),
            pltpu.VMEM((chunks,) + shape, dtype),
            pltpu.SemaphoreType.DMA((chunks + 1,)),
        ],
        compiler_params=params(40),
        cost_estimate=pl.CostEstimate(
            flops=2 * 9 * channels * states * width * CHUNK * chunks,
            bytes_accessed=2 * total * channels * width + weight.size * 2,
            transcendentals=0,
        ),
        name="conv_chunks",
    )(*operands)


def pair_kernel(keep, other, coefs, out):
    for q in range(CHUNK):
        out[q] = coefs[:, 2:3] * keep[q] + coefs[:, 3:4] * other[q].astype(jnp.float32)


def pair_drive(keep, other, coefs):
    return pl.pallas_call(
        pair_kernel,
        out_shape=jax.ShapeDtypeStruct(keep.shape, jnp.float32),
        in_specs=[VMEM] * 3,
        out_specs=VMEM,
        compiler_params=params(8),
        name="pair_drive",
    )(keep, other, coefs)


def pick(place, values, q):
    out = values[-1][q]
    for j in range(len(values) - 1):
        out = jnp.where(place[0] == j, values[j][q], out)
    return out.astype(jnp.float32)


def carry_kernel(drives, with_carry, place, coefs, *refs):
    out = refs[-1]
    for q in range(CHUNK):
        total = pick(place, refs[:drives], q)
        if with_carry:
            total = total + coefs[:, 1:2] * refs[drives][q].astype(jnp.float32)
        out[q] = total.astype(jnp.bfloat16)


def carry_on(place, coefs, drives, carry):
    operands = list(drives) + ([carry] if carry is not None else [])
    return pl.pallas_call(
        functools.partial(carry_kernel, len(drives), carry is not None),
        out_shape=jax.ShapeDtypeStruct(drives[0].shape, jnp.bfloat16),
        in_specs=[SMEM, VMEM] + [VMEM] * len(operands),
        out_specs=VMEM,
        compiler_params=params(16),
        name="carry_on",
    )(place, coefs, *operands)


def states_kernel(place, coefs, keep, other, *refs):
    carries, (own, back) = refs[:-2], refs[-2:]
    for q in range(CHUNK):
        held, sent = keep[q], other[q].astype(jnp.float32)
        carry = pick(place, carries, q)
        own[q] = (held + coefs[:, 5:6] * sent + coefs[:, 4:5] * carry).astype(jnp.bfloat16)
        back[q] = (coefs[:, 7:8] * held + sent + coefs[:, 6:7] * carry).astype(jnp.bfloat16)


def states_of(place, coefs, keep, other, carries):
    out = jax.ShapeDtypeStruct(keep.shape, jnp.bfloat16)
    return pl.pallas_call(
        states_kernel,
        out_shape=[out, out],
        in_specs=[SMEM] + [VMEM] * (3 + len(carries)),
        out_specs=[VMEM, VMEM],
        compiler_params=params(16),
        name="states_of",
    )(place, coefs, keep, other, *carries)


def output_kernel(chunks, place, rows_in, weight, skip, *refs):
    states, (out, held, total, sems) = refs[:-4], refs[-4:]
    channels, tile_rows, width = out.shape
    for n, chunk in enumerate(states):
        pltpu.make_async_copy(chunk, held.at[n], sems.at[n]).start()
    for n, chunk in enumerate(states):
        pltpu.make_async_copy(chunk, held.at[n], sems.at[n]).wait()
    gain = skip[:, 0:1]

    def one(n, _):
        second = n // chunks
        k = n - second * chunks
        r = jnp.where(second == 0, place[0] + k * place[1], place[2] + k * place[3])
        value = jnp.dot(
            weight[...],
            jnp.concatenate([held[n, q] for q in range(CHUNK)], axis=1),
            preferred_element_type=jnp.float32,
        )
        for q in range(CHUNK):
            total[pl.ds(r + q, channels, stride=tile_rows), :] = value[
                :, q * width : (q + 1) * width
            ] + gain * rows_in[r + q].astype(jnp.float32)
        return _

    lax.fori_loop(0, 2 * chunks, one, 0)
    block = 16

    def settle(n, _):
        values = total[pl.ds(pl.multiple_of(n * block * tile_rows, 8), block * tile_rows), :]
        out[pl.ds(n * block, block)] = values.reshape(block, tile_rows, width).astype(out.dtype)
        return _

    lax.fori_loop(0, channels // block, settle, 0)


def output_of(place, rows_in, weight, skip, states, chunks, dtype):
    tile_rows, channels, width = rows_in.shape
    return pl.pallas_call(
        functools.partial(output_kernel, chunks),
        out_shape=jax.ShapeDtypeStruct((channels, tile_rows, width), dtype),
        in_specs=[SMEM] + [VMEM] * 3 + [ANY] * len(states),
        out_specs=VMEM,
        scratch_shapes=[
            pltpu.VMEM((len(states),) + states[0].shape, states[0].dtype),
            pltpu.VMEM((channels * tile_rows, width), jnp.float32),
            pltpu.SemaphoreType.DMA((len(states),)),
        ],
        compiler_params=params(40),
        name="output_of",
    )(place, rows_in, weight, skip, *states)


def on_device(frames_in, conv_weight, out_weight, skip_gain, decays):
    tile_rows = frames_in.shape[2]
    frames = lax.axis_size("tm")
    spaces = lax.axis_size("space")
    groups = frames // 2
    me = lax.axis_index("tm")
    group, odd = me // 2, me % 2
    even = odd == 0
    half = tile_rows // 2
    chunks = half // CHUNK
    swap = [(i, i + 1 - 2 * (i % 2)) for i in range(frames)]
    onward = [(i, i + 2) for i in range(frames - 2)]
    down = [(i, i + 1) for i in range(spaces - 1)]
    up = [(i + 1, i) for i in range(spaces - 1)]

    rows = jnp.transpose(frames_in[0], (1, 0, 2))
    own_decay = decays[0]
    other_decay = lax.ppermute(own_decay, "tm", swap)
    from_low = lax.ppermute(rows[tile_rows - 1], "space", down)
    from_high = lax.ppermute(rows[0], "space", up)

    gain = jnp.sqrt(1.0 - own_decay * own_decay)
    decay_even = jnp.where(even, own_decay, other_decay)
    decay_odd = jnp.where(even, other_decay, own_decay)
    later = jnp.where(group > 0, 1.0, 0.0)
    both = decay_even * decay_odd * later
    first = decay_even * later
    one, zero = jnp.ones_like(gain), jnp.zeros_like(gain)
    coefs = jnp.stack(
        [
            gain,
            both,
            jnp.where(even, decay_odd, one),
            jnp.where(even, one, decay_odd),
            jnp.where(even, first, both),
            jnp.where(even, zero, decay_odd),
            jnp.where(even, both, first),
            jnp.where(even, decay_odd, zero),
        ],
        axis=1,
    )
    gains = jnp.stack([gain] * 8, axis=1)

    def place_of(lower, start, count):
        whole = start + count == chunks
        top = jnp.where(lower, half + CHUNK * start, half - CHUNK * (start + count)) - 1
        if whole:
            top = jnp.where(lower, top, 0)
            slot = jnp.where(lower, 0, 1)
        else:
            slot = jnp.zeros((), jnp.int32)
        step = jnp.where(lower, CHUNK, -CHUNK)
        begin = jnp.where(lower, 0, CHUNK * (count - 1))
        halo = jnp.where(lower, CHUNK * count + 1, 0)
        return jnp.stack([top, slot, step, begin, halo]).astype(jnp.int32)

    halo_sent = jnp.where(even, from_high, from_low)
    halo_kept = jnp.where(even, from_low, from_high)
    send = conv(
        rows, None, conv_weight, gains, place_of(even, 0, FIRST), FIRST, jnp.bfloat16
    )
    send += conv(
        rows, halo_sent, conv_weight, gains,
        place_of(even, FIRST, chunks - FIRST), chunks - FIRST, jnp.bfloat16,
    )
    kept = conv(
        rows, halo_kept, conv_weight, gains, place_of(~even, 0, chunks), chunks, jnp.float32
    )
    others = [lax.ppermute(value, "tm", swap) for value in send]

    where = jnp.stack([group, group - 1]).astype(jnp.int32)
    carries, drives, own, back = [], [], [], []
    for step in range(chunks + groups - 1):
        if step < chunks:
            drives.append(pair_drive(kept[step], others[step], coefs))
        if step < chunks + groups - 2:
            ready = [
                drives[min(max(step - g, 0), chunks - 1)] for g in range(groups)
            ]
            sum_out = carry_on(where[:1], coefs, ready, carries[-1] if carries else None)
            carries.append(lax.ppermute(sum_out, "tm", onward))
        k = step - (groups - 1)
        if k >= 0:
            mine, theirs = states_of(
                where[1:], coefs, kept[k], others[k], carries[k : k + groups - 1]
            )
            own.append(mine)
            back.append(lax.ppermute(theirs, "tm", swap))

    place = jnp.where(
        even,
        jnp.array([half - CHUNK, -CHUNK, half, CHUNK], jnp.int32),
        jnp.array([half, CHUNK, half - CHUNK, -CHUNK], jnp.int32),
    )
    skip = jnp.stack([skip_gain] * 8, axis=1)
    result = output_of(place, rows, out_weight, skip, own + back, chunks, frames_in.dtype)
    return result[None]


def solution(mesh):
    placed = (P("tm", None, "space", None), P(), P(), P(), P("tm", None))
    return jax.shard_map(
        on_device,
        mesh=mesh,
        in_specs=placed,
        out_specs=P("tm", None, "space", None),
        check_vma=False,
    )
```

```python
import functools

import jax
import jax.numpy as jnp
from jax import lax
from jax.experimental import pallas as pl
from jax.experimental.pallas import tpu as pltpu
from jax.sharding import PartitionSpec as P

MIB = 1 << 20
VMEM = pl.BlockSpec(memory_space=pltpu.VMEM)
ANY = pl.BlockSpec(memory_space=pl.ANY)
SMEM = pl.BlockSpec(memory_space=pltpu.SMEM)
BF16, F32 = jnp.bfloat16, jnp.float32


def params(mib):
    return pltpu.CompilerParams(vmem_limit_bytes=mib * MIB)


def sizes_of(half):
    if half % 4 or half < 8:
        return [2] * (half // 2)
    return [2] + [4] * (half // 4 - 1) + [2]


def columns(*rows):
    rows = list(rows) + [rows[0]] * (8 - len(rows))
    return jnp.transpose(jnp.concatenate(rows, axis=0))


def call(kernel, out_shape, scalars, operands, after, name, mib=16, scratch=(), specs=None, **more):
    specs = specs or [VMEM] * len(operands)
    n = len(scalars) + len(operands)

    def body(*refs):
        kernel(*refs[:n], *refs[n + len(after) :])

    return pl.pallas_call(
        body,
        out_shape=out_shape,
        in_specs=[SMEM] * len(scalars) + specs + [ANY] * len(after),
        scratch_shapes=list(scratch),
        compiler_params=params(mib),
        name=name,
        **more,
    )(*scalars, *operands, *after)


def conv(rows_in, halo, weight, decays, lower, edge, sizes, start, count, dtype, after, edges=False):
    tile_rows, channels, width = rows_in.shape
    states = weight.shape[2]
    half = tile_rows // 2
    mine = sizes[start : start + count]
    before, total = sum(sizes[:start]), sum(mine)
    whole = start + count == len(sizes)
    assert whole == (halo is not None)
    out_shape = [jax.ShapeDtypeStruct((n, states, width), dtype) for n in mine]
    if edges:
        out_shape += [jax.ShapeDtypeStruct((channels, width), rows_in.dtype)] * 2
        out_shape += [jax.ShapeDtypeStruct(decays.shape, decays.dtype)]

    def kernel(lower_ref, edge_ref, rows_ref, weight_ref, decays_ref, *refs):
        refs = list(refs)
        halo_ref = refs.pop(0) if whole else None
        outs, (rows, shifted, sems) = refs[:-3], refs[-3:]
        low = lower_ref[0]
        copied = total + 1 if whole else total + 2
        first_low = half + before - 1
        first_up = 0 if whole else half - before - total - 1
        main = pltpu.make_async_copy(
            rows_ref.at[pl.ds(first_up + low * (first_low - first_up), copied)],
            rows.at[pl.ds((1 - low) if whole else 0, copied)],
            sems.at[0],
        )
        main.start()
        if edges:
            top = pltpu.make_async_copy(rows_ref.at[0], outs[count], sems.at[1])
            bottom = pltpu.make_async_copy(rows_ref.at[tile_rows - 1], outs[count + 1], sems.at[2])
            top.start()
            bottom.start()
            outs[count + 2][...] = decays_ref[...]
        main.wait()
        if whole:
            slot = low * (total + 1)
            rows[slot] = jnp.where(edge_ref[0] == 1, jnp.zeros_like(halo_ref), halo_ref[...])
        lane = lax.broadcasted_iota(jnp.int32, (channels, width), 1)

        def shift(r, carry):
            row = rows[r].astype(F32)
            left = jnp.where(lane == 0, 0.0, pltpu.roll(row, 1, 1))
            right = jnp.where(lane == width - 1, 0.0, pltpu.roll(row, width - 1, 1))
            shifted[r, :channels] = left.astype(rows.dtype)
            shifted[r, channels : 2 * channels] = rows[r]
            shifted[r, 2 * channels :] = right.astype(rows.dtype)
            return carry

        lax.fori_loop(0, total + 2, shift, 0, unroll=2)
        decay = decays_ref[...]
        gain = columns(jnp.sqrt(1.0 - decay * decay))[:, 0:1]
        taps = jnp.concatenate([weight_ref[i, j] for i in range(3) for j in range(3)], axis=1)
        done = 0
        for n, size in enumerate(mine):
            at_low, at_up = done, total - done - size
            for q in range(0, size, 2):
                r = at_up + q + low * (at_low - at_up)
                window = jnp.concatenate(
                    [
                        jnp.concatenate([shifted[r + i], shifted[r + i + 1]], axis=1)
                        for i in range(3)
                    ],
                    axis=0,
                )
                drive = gain * jnp.dot(taps, window, preferred_element_type=F32)
                outs[n][q] = drive[:, :width].astype(dtype)
                outs[n][q + 1] = drive[:, width:].astype(dtype)
            done += size
        if edges:
            top.wait()
            bottom.wait()

    out_specs = [VMEM] * count + ([ANY, ANY, VMEM] if edges else [])
    return call(
        kernel, out_shape, [lower, edge],
        [rows_in, weight, decays] + ([halo] if whole else []), after, "conv_chunks", 40,
        scratch=[
            pltpu.VMEM((total + 2, channels, width), rows_in.dtype),
            pltpu.VMEM((total + 2, 3 * channels, width), rows_in.dtype),
            pltpu.SemaphoreType.DMA((3,)),
        ],
        specs=[ANY, VMEM, VMEM] + ([VMEM] if whole else []),
        out_specs=out_specs,
        cost_estimate=pl.CostEstimate(
            flops=18 * channels * states * width * total,
            bytes_accessed=4 * total * channels * width + weight.size * 2,
            transcendentals=0,
        ),
    )


def coefficients(odd, own_decay, other_decay, after):
    def kernel(odd_ref, own_ref, other_ref, out):
        is_odd = jnp.full(own_ref.shape, odd_ref[0], jnp.int32) == 1
        own, other = own_ref[...], other_ref[...]
        both = own * other
        one, zero = jnp.ones_like(own), jnp.zeros_like(own)
        out[...] = columns(
            both,
            jnp.where(is_odd, one, other),
            jnp.where(is_odd, own, one),
            jnp.where(is_odd, both, own),
            jnp.where(is_odd, other, both),
            jnp.where(is_odd, own, zero),
            jnp.where(is_odd, zero, other),
        )

    shape = jax.ShapeDtypeStruct((own_decay.shape[1], 8), F32)
    return call(kernel, shape, [odd], [own_decay, other_decay], after, "coefficients")


def pair_drive(keep, other, coefs, after):
    def kernel(keep_ref, other_ref, coefs_ref, out):
        for q in range(keep.shape[0]):
            out[q] = coefs_ref[:, 1:2] * keep_ref[q] + coefs_ref[:, 2:3] * other_ref[q].astype(F32)

    shape = jax.ShapeDtypeStruct(keep.shape, F32)
    return call(kernel, shape, [], [keep, other, coefs], after, "pair_drive")


def carry_on(group, coefs, drives, carry, after):
    groups = sorted(drives)
    most = max(drives[g].shape[0] for g in groups)
    shape = jax.ShapeDtypeStruct((most,) + drives[groups[0]].shape[1:], BF16)

    def kernel(group_ref, coefs_ref, *refs):
        out = refs[-1]
        out[...] = jnp.zeros_like(out)
        for g, ref in zip(groups, refs):

            @pl.when(group_ref[0] == g)
            def one(g=g, ref=ref):
                for q in range(ref.shape[0]):
                    total = ref[q]
                    if g > 0:
                        total = total + coefs_ref[:, 0:1] * refs[len(groups)][q].astype(F32)
                    out[q] = total.astype(BF16)

    operands = [coefs] + [drives[g] for g in groups] + ([carry] if carry is not None else [])
    return call(kernel, shape, [group], operands, after, "carry_on")


def states_of(group, coefs, keep, other, carries, after):
    shape = jax.ShapeDtypeStruct(keep.shape, BF16)

    def kernel(group_ref, coefs_ref, keep_ref, other_ref, *refs):
        own, back = refs[-2:]

        def settle(carry_ref):
            for q in range(keep.shape[0]):
                held, sent = keep_ref[q], other_ref[q].astype(F32)
                mine = held + coefs_ref[:, 5:6] * sent
                theirs = coefs_ref[:, 6:7] * held + sent
                if carry_ref is not None:
                    carry = carry_ref[q].astype(F32)
                    mine = mine + coefs_ref[:, 3:4] * carry
                    theirs = theirs + coefs_ref[:, 4:5] * carry
                own[q] = mine.astype(BF16)
                back[q] = theirs.astype(BF16)

        for g in range(len(carries) + 1):
            pl.when(group_ref[0] == g)(functools.partial(settle, refs[g - 1] if g else None))

    return call(
        kernel, [shape, shape], [group], [coefs, keep, other] + list(carries), after, "states_of"
    )


def output_half(lower, rows_in, weight, skip, states, earlier, after, dtype):
    tile_rows, channels, width = rows_in.shape
    half = tile_rows // 2
    pitch = channels + 1
    count = len(states)
    sizes = [value.shape[0] for value in states]

    def kernel(lower_ref, rows_ref, weight_ref, skip_ref, *refs):
        chunks = refs[:count]
        out, rows, held, total, tile, sems = refs[-6:]
        low = lower_ref[0]
        begin = pl.multiple_of(low * half, half)
        main = pltpu.make_async_copy(rows_ref.at[pl.ds(begin, half)], rows, sems.at[0])
        main.start()
        copies = []
        done = 0
        for n, chunk in enumerate(chunks):
            at_up = half - done - sizes[n]
            r = at_up + low * (done - at_up)
            copies.append(
                pltpu.make_async_copy(chunk, held.at[pl.ds(r, sizes[n])], sems.at[n + 1])
            )
            done += sizes[n]
        for copy in copies:
            copy.start()
        gain = columns(skip_ref[...])[:, 0:1]
        main.wait()
        for copy in copies:
            copy.wait()

        def one(p, carry):
            r = 2 * p
            value = jnp.dot(
                weight_ref[...],
                jnp.concatenate([held[r], held[r + 1]], axis=1),
                preferred_element_type=F32,
            )
            for q in range(2):
                total[pl.ds((r + q) * pitch, channels), :] = value[
                    :, q * width : (q + 1) * width
                ] + gain * rows[r + q].astype(F32)
            return carry

        lax.fori_loop(0, half // 2, one, 0)

        def settle(n, carry):
            for i in range(8):
                tile[n * 8 + i] = total[pl.ds(n * 8 + i, half, stride=pitch), :].astype(dtype)
            return carry

        lax.fori_loop(0, channels // 8, settle, 0, unroll=2)
        last = pltpu.make_async_copy(tile, out.at[:, pl.ds(begin, half), :], sems.at[count + 1])
        last.start()
        last.wait()

    operands = [rows_in, weight, skip] + list(states)
    more = {}
    if earlier is not None:
        operands.append(earlier)
        more["input_output_aliases"] = {len(operands): 0}
    return call(
        kernel,
        jax.ShapeDtypeStruct((channels, tile_rows, width), dtype),
        [lower], operands, after, "output_half", 40,
        scratch=[
            pltpu.VMEM((half, channels, width), rows_in.dtype),
            pltpu.VMEM((half, channels, width), BF16),
            pltpu.VMEM((half * pitch + 8, width), F32),
            pltpu.VMEM((channels, half, width), dtype),
            pltpu.SemaphoreType.DMA((count + 2,)),
        ],
        specs=[ANY, VMEM, VMEM] + [ANY] * (len(operands) - 3),
        out_specs=ANY,
        **more,
    )


def on_device(frames_in, conv_weight, out_weight, skip_gain, decays):
    tile_rows = frames_in.shape[2]
    frames = lax.axis_size("tm")
    spaces = lax.axis_size("space")
    groups = frames // 2
    me, at = lax.axis_index("tm"), lax.axis_index("space")
    scalar = lambda value: jnp.asarray(value, jnp.int32).reshape(1)
    group, odd, even = scalar(me // 2), scalar(me % 2), scalar(1 - me % 2)
    is_top, is_bottom = scalar(at == 0), scalar(at == spaces - 1)
    is_even = me % 2 == 0
    sizes = sizes_of(tile_rows // 2)
    chunks = len(sizes)

    swap = [(i, i + 1 - 2 * (i % 2)) for i in range(frames)]
    even_hop = [(i, i + 2 if (i // 2) % 2 == 0 else i - 2) for i in range(frames)]
    odd_hop = [
        (i, i if i // 2 in (0, groups - 1) else (i + 2 if (i // 2) % 2 else i - 2))
        for i in range(frames)
    ]
    down = [(i, (i + 1) % spaces) for i in range(spaces)]
    up = [(i, (i - 1) % spaces) for i in range(spaces)]

    rows = jnp.transpose(frames_in[0], (1, 0, 2))
    sent = functools.partial(
        conv, rows, weight=conv_weight, decays=decays, lower=even,
        edge=jnp.where(is_even, is_bottom, is_top), sizes=sizes, dtype=BF16,
    )
    kept = functools.partial(
        conv, rows, weight=conv_weight, decays=decays, lower=odd,
        edge=jnp.where(is_even, is_top, is_bottom), sizes=sizes, dtype=F32,
    )
    first, top, bottom, decay = sent(halo=None, start=0, count=1, after=[], edges=True)
    others = [lax.ppermute(first, "tm", swap)]
    other_decay = lax.ppermute(decay, "tm", swap)
    from_low = lax.ppermute(bottom, "space", down)
    from_high = lax.ppermute(top, "space", up)
    halo_sent = jnp.where(is_even, from_high, from_low)
    halo_kept = jnp.where(is_even, from_low, from_high)
    rest = sent(halo=halo_sent, start=1, count=chunks - 1, after=[])
    others += [lax.ppermute(value, "tm", swap) for value in rest]
    held = list(kept(halo=None, start=0, count=1, after=[rest[-1]]))
    coefs = coefficients(odd, decays, other_decay, [held[-1]])

    lag = 3 * ((groups - 2) // 2) + 1
    drives, evens, odds, own, back = [], {}, {}, [], []
    drives.append(pair_drive(held[0], others[0], coefs, []))
    after = [drives[0]]
    for step in range(chunks + lag):
        ready = {
            g: drives[step - 3 * (g // 2)]
            for g in range(0, groups - 1, 2)
            if 0 <= step - 3 * (g // 2) < chunks
        }
        if ready:
            value = carry_on(group, coefs, ready, odds.get(step - 2), after)
            evens[step] = lax.ppermute(value, "tm", even_hop)
            after = [value]
        if step == 0:
            held += kept(halo=halo_kept, start=1, count=chunks - 1, after=after)
            after = [held[-1]]
        k = step - lag
        if k >= 0:
            carries = [
                evens[k + 3 * ((g - 1) // 2)] if g % 2 else odds[k + 1 + 3 * ((g - 2) // 2)]
                for g in range(1, groups)
            ]
            mine, theirs = states_of(group, coefs, held[k], others[k], carries, after)
            own.append(mine)
            back.append(lax.ppermute(theirs, "tm", swap))
            after = [theirs]
        ready = {
            g: drives[step - 1 - 3 * ((g - 1) // 2)]
            for g in range(1, groups - 1, 2)
            if 0 <= step - 1 - 3 * ((g - 1) // 2) < chunks
        }
        if ready:
            value = carry_on(group, coefs, ready, evens[step - 1], after)
            odds[step] = lax.ppermute(value, "tm", odd_hop)
            after = [value]
        if step + 1 < chunks:
            drives.append(pair_drive(held[step + 1], others[step + 1], coefs, after))
            after = [drives[-1]]

    skip = skip_gain[None]
    dtype = frames_in.dtype
    half_done = output_half(odd, rows, out_weight, skip, own, None, after, dtype)
    result = output_half(even, rows, out_weight, skip, back, half_done, [], dtype)
    return result[None]


def solution(mesh):
    placed = (P("tm", None, "space", None), P(), P(), P(), P("tm", None))
    return jax.shard_map(
        on_device,
        mesh=mesh,
        in_specs=placed,
        out_specs=P("tm", None, "space", None),
        check_vma=False,
    )
```

```python
import functools

import jax
import jax.numpy as jnp
from jax import lax
from jax.experimental import pallas as pl
from jax.experimental.pallas import tpu as pltpu
from jax.sharding import PartitionSpec as P

MIB = 1 << 20
VMEM = pl.BlockSpec(memory_space=pltpu.VMEM)
ANY = pl.BlockSpec(memory_space=pl.ANY)
SMEM = pl.BlockSpec(memory_space=pltpu.SMEM)
BF16, F32 = jnp.bfloat16, jnp.float32


def params(mib):
    return pltpu.CompilerParams(vmem_limit_bytes=mib * MIB)


def sizes_of(half):
    rows = 4 if half % 4 == 0 else 2
    return [rows] * (half // rows)


def row(ref, q, channels):
    return ref[q * channels : (q + 1) * channels] if len(ref.shape) == 2 else ref[q]


PAD = 16
LANES = 128


def split_decays(decay):
    pieces = []
    rest = decay
    for _ in range(3):
        part = rest.astype(BF16).astype(F32)
        rest = rest - part
        pieces += [part[:, i : i + LANES] for i in range(0, decay.shape[1], LANES)]
    pieces += [jnp.zeros_like(pieces[0])] * (PAD - len(pieces))
    return jnp.concatenate(pieces, axis=0).astype(BF16)


def join_decays(block, count):
    block = block.astype(F32)
    n = count // LANES
    parts = [block[i : i + 1] + block[n + i : n + i + 1] + block[2 * n + i : 2 * n + i + 1] for i in range(n)]
    return jnp.concatenate(parts, axis=1)


def columns(*rows):
    rows = list(rows) + [rows[0]] * (8 - len(rows))
    return jnp.transpose(jnp.concatenate(rows, axis=0))


TOKEN = jax.ShapeDtypeStruct((8, 128), F32)


def call(kernel, out_shape, scalars, operands, after, name, mib=8, scratch=(), specs=None,
         out_specs=None, **more):
    specs = specs or [VMEM] * len(operands)
    out_specs = out_specs or [VMEM] * len(out_shape)
    n, outs = len(scalars) + len(operands), len(out_shape)

    def body(*refs):
        rest = refs[n + len(after) :]
        rest[outs][...] = jnp.zeros(TOKEN.shape, TOKEN.dtype)
        kernel(*refs[:n], *rest[:outs], *rest[outs + 1 :])

    return pl.pallas_call(
        body,
        out_shape=list(out_shape) + [TOKEN],
        in_specs=[SMEM] * len(scalars) + specs + [ANY] * len(after),
        out_specs=list(out_specs) + [VMEM],
        scratch_shapes=list(scratch),
        compiler_params=params(mib),
        cost_estimate=pl.CostEstimate(flops=1, bytes_accessed=1, transcendentals=0),
        name=name,
        **more,
    )(*scalars, *operands, *after)


def conv(rows_in, halos, weight, decays, lower, edge, sizes, start, count, dtype, after, edges=False):
    tile_rows, channels, width = rows_in.shape
    states = weight.shape[2]
    half = tile_rows // 2
    mine = sizes[start : start + count]
    before, total = sum(sizes[:start]), sum(mine)
    whole = start + count == len(sizes)
    assert whole == bool(halos)
    out_shape = [jax.ShapeDtypeStruct((n, states, width), dtype) for n in mine]
    if edges:
        out_shape += [jax.ShapeDtypeStruct((channels, width), rows_in.dtype)] * 2
        out_shape[0] = jax.ShapeDtypeStruct((mine[0] * states + PAD, width), dtype)

    def kernel(lower_ref, edge_ref, rows_ref, weight_ref, decays_ref, *refs):
        refs = list(refs)
        above, below = (refs.pop(0), refs.pop(0)) if whole else (None, None)
        outs, (rows, shifted, sems) = refs[:-3], refs[-3:]
        low = lower_ref[0]
        copied = total + 1 if whole else total + 2
        first_low = half + before - 1
        first_up = 0 if whole else half - before - total - 1
        main = pltpu.make_async_copy(
            rows_ref.at[pl.ds(first_up + low * (first_low - first_up), copied)],
            rows.at[pl.ds((1 - low) if whole else 0, copied)],
            sems.at[0],
        )
        main.start()
        if edges:
            top = pltpu.make_async_copy(rows_ref.at[0], outs[count], sems.at[1])
            bottom = pltpu.make_async_copy(rows_ref.at[tile_rows - 1], outs[count + 1], sems.at[2])
            top.start()
            bottom.start()
            outs[0][mine[0] * states :] = split_decays(decays_ref[...])
        main.wait()
        if whole:
            slot = low * (total + 1)
            halo = jnp.where(low == 1, below[...].astype(F32), above[...].astype(F32))
            rows[slot] = jnp.where(edge_ref[0] == 1, 0.0, halo).astype(rows.dtype)
        lane = lax.broadcasted_iota(jnp.int32, (channels, width), 1)

        def shift(r, carry):
            row = rows[r].astype(F32)
            left = jnp.where(lane == 0, 0.0, pltpu.roll(row, 1, 1))
            right = jnp.where(lane == width - 1, 0.0, pltpu.roll(row, width - 1, 1))
            shifted[r, :channels] = left.astype(rows.dtype)
            shifted[r, channels : 2 * channels] = rows[r]
            shifted[r, 2 * channels :] = right.astype(rows.dtype)
            return carry

        lax.fori_loop(0, total + 2, shift, 0, unroll=2)
        decay = decays_ref[...]
        gain = columns(jnp.sqrt(1.0 - decay * decay))[:, 0:1]
        taps = jnp.concatenate([weight_ref[i, j] for i in range(3) for j in range(3)], axis=1)
        done = 0
        for n, size in enumerate(mine):
            at_low, at_up = done, total - done - size
            for q in range(0, size, 2):
                r = at_up + q + low * (at_low - at_up)
                window = jnp.concatenate(
                    [
                        jnp.concatenate([shifted[r + i], shifted[r + i + 1]], axis=1)
                        for i in range(3)
                    ],
                    axis=0,
                )
                drive = gain * jnp.dot(taps, window, preferred_element_type=F32)
                for i in range(2):
                    value = drive[:, i * width : (i + 1) * width].astype(dtype)
                    if len(outs[n].shape) == 2:
                        outs[n][(q + i) * states : (q + i + 1) * states] = value
                    else:
                        outs[n][q + i] = value
            done += size
        if edges:
            top.wait()
            bottom.wait()

    out_specs = [VMEM] * count + ([ANY, ANY] if edges else [])
    return call(
        kernel, out_shape, [lower, edge],
        [rows_in, weight, decays] + list(halos), after, "conv_chunks", 14,
        scratch=[
            pltpu.VMEM((total + 2, channels, width), rows_in.dtype),
            pltpu.VMEM((total + 2, 3 * channels, width), rows_in.dtype),
            pltpu.SemaphoreType.DMA((3,)),
        ],
        specs=[ANY, VMEM, VMEM] + [VMEM] * len(halos),
        out_specs=out_specs,
    )


def coefficients(odd, own_decay, first, after):
    def kernel(odd_ref, own_ref, first_ref, out):
        is_odd = jnp.full(own_ref.shape, odd_ref[0], jnp.int32) == 1
        own = own_ref[...]
        other = join_decays(first_ref[first.shape[0] - PAD :], own.shape[1])
        both = own * other
        one, zero = jnp.ones_like(own), jnp.zeros_like(own)
        out[...] = columns(
            both,
            jnp.where(is_odd, one, other),
            jnp.where(is_odd, own, one),
            jnp.where(is_odd, both, own),
            jnp.where(is_odd, other, both),
            jnp.where(is_odd, own, zero),
            jnp.where(is_odd, zero, other),
        )

    shape = jax.ShapeDtypeStruct((own_decay.shape[1], 8), F32)
    return call(kernel, [shape], [odd], [own_decay, first], after, "coefficients")


def pair_drive(keep, other, coefs, after):
    def kernel(keep_ref, other_ref, coefs_ref, out):
        for q in range(keep.shape[0]):
            out[q] = coefs_ref[:, 1:2] * keep_ref[q] + coefs_ref[:, 2:3] * row(
                other_ref, q, keep.shape[1]
            ).astype(F32)

    shape = jax.ShapeDtypeStruct(keep.shape, F32)
    return call(kernel, [shape], [], [keep, other, coefs], after, "pair_drive")


def carry_on(group, coefs, drives, carry, after):
    groups = sorted(drives)
    most = max(drives[g].shape[0] for g in groups)
    shape = jax.ShapeDtypeStruct((most,) + drives[groups[0]].shape[1:], BF16)

    def kernel(group_ref, coefs_ref, *refs):
        out = refs[-1]
        out[...] = jnp.zeros_like(out)
        for g, ref in zip(groups, refs):

            @pl.when(group_ref[0] == g)
            def one(g=g, ref=ref):
                for q in range(ref.shape[0]):
                    total = ref[q]
                    if g > 0:
                        total = total + coefs_ref[:, 0:1] * refs[len(groups)][q].astype(F32)
                    out[q] = total.astype(BF16)

    operands = [coefs] + [drives[g] for g in groups] + ([carry] if carry is not None else [])
    return call(kernel, [shape], [group], operands, after, "carry_on")


def states_of(group, coefs, keep, other, carries, after):
    shape = jax.ShapeDtypeStruct(keep.shape, BF16)

    def kernel(group_ref, coefs_ref, keep_ref, other_ref, *refs):
        own, back = refs[-2:]

        def settle(carry_ref):
            for q in range(keep.shape[0]):
                held, sent = keep_ref[q], row(other_ref, q, keep.shape[1]).astype(F32)
                mine = held + coefs_ref[:, 5:6] * sent
                theirs = coefs_ref[:, 6:7] * held + sent
                if carry_ref is not None:
                    carry = carry_ref[q].astype(F32)
                    mine = mine + coefs_ref[:, 3:4] * carry
                    theirs = theirs + coefs_ref[:, 4:5] * carry
                own[q] = mine.astype(BF16)
                back[q] = theirs.astype(BF16)

        for g in range(len(carries) + 1):
            pl.when(group_ref[0] == g)(functools.partial(settle, refs[g - 1] if g else None))

    return call(
        kernel, [shape, shape], [group], [coefs, keep, other] + list(carries), after, "states_of"
    )


def output_half(lower, rows_in, weight, skip, states, earlier, after, dtype):
    tile_rows, channels, width = rows_in.shape
    half = tile_rows // 2
    pitch = channels + 1
    count = len(states)
    sizes = [value.shape[0] for value in states]

    def kernel(lower_ref, rows_ref, weight_ref, skip_ref, *refs):
        chunks = refs[:count]
        out, rows, held, total, tile, sems = refs[-6:]
        low = lower_ref[0]
        begin = pl.multiple_of(low * half, half)
        main = pltpu.make_async_copy(rows_ref.at[pl.ds(begin, half)], rows, sems.at[0])
        main.start()
        copies = []
        done = 0
        for n, chunk in enumerate(chunks):
            at_up = half - done - sizes[n]
            r = at_up + low * (done - at_up)
            copies.append(
                pltpu.make_async_copy(chunk, held.at[pl.ds(r, sizes[n])], sems.at[n + 1])
            )
            done += sizes[n]
        for copy in copies:
            copy.start()
        gain = columns(skip_ref[...])[:, 0:1]
        main.wait()
        for copy in copies:
            copy.wait()

        def one(p, carry):
            r = 2 * p
            value = jnp.dot(
                weight_ref[...],
                jnp.concatenate([held[r], held[r + 1]], axis=1),
                preferred_element_type=F32,
            )
            for q in range(2):
                total[pl.ds((r + q) * pitch, channels), :] = value[
                    :, q * width : (q + 1) * width
                ] + gain * rows[r + q].astype(F32)
            return carry

        lax.fori_loop(0, half // 2, one, 0)

        def settle(n, carry):
            for i in range(8):
                tile[n * 8 + i] = total[pl.ds(n * 8 + i, half, stride=pitch), :].astype(dtype)
            return carry

        lax.fori_loop(0, channels // 8, settle, 0, unroll=2)
        last = pltpu.make_async_copy(tile, out.at[:, pl.ds(begin, half), :], sems.at[count + 1])
        last.start()
        last.wait()

    operands = [rows_in, weight, skip] + list(states)
    more = {}
    if earlier is not None:
        operands.append(earlier)
        more["input_output_aliases"] = {len(operands): 0}
    return call(
        kernel,
        [jax.ShapeDtypeStruct((channels, tile_rows, width), dtype)],
        [lower], operands, after, "output_half", 10,
        scratch=[
            pltpu.VMEM((half, channels, width), rows_in.dtype),
            pltpu.VMEM((half, channels, width), BF16),
            pltpu.VMEM((half * pitch + 8, width), F32),
            pltpu.VMEM((channels, half, width), dtype),
            pltpu.SemaphoreType.DMA((count + 2,)),
        ],
        specs=[ANY, VMEM, VMEM] + [ANY] * (len(operands) - 3),
        out_specs=[ANY],
        **more,
    )


def on_device(frames_in, conv_weight, out_weight, skip_gain, decays):
    tile_rows = frames_in.shape[2]
    frames = lax.axis_size("tm")
    spaces = lax.axis_size("space")
    groups = frames // 2
    me, at = lax.axis_index("tm"), lax.axis_index("space")
    scalar = lambda value: jnp.asarray(value, jnp.int32).reshape(1)
    group, odd, even = scalar(me // 2), scalar(me % 2), scalar(1 - me % 2)
    is_top, is_bottom = scalar(at == 0), scalar(at == spaces - 1)
    is_even = me % 2 == 0
    sizes = sizes_of(tile_rows // 2)
    chunks = len(sizes)

    swap = [(i, i + 1 - 2 * (i % 2)) for i in range(frames)]
    even_hop = [(i, i + 2 if (i // 2) % 2 == 0 else i - 2) for i in range(frames)]
    odd_hop = [
        (i * spaces + j, i * spaces + j + 1 - 2 * (j % 2))
        if i // 2 in (0, groups - 1)
        else (i * spaces + j, (i + 2 if (i // 2) % 2 else i - 2) * spaces + j)
        for i in range(frames)
        for j in range(spaces)
    ]
    down = [(i, (i + 1) % spaces) for i in range(spaces)]
    up = [(i, (i - 1) % spaces) for i in range(spaces)]

    rows = jnp.transpose(frames_in[0], (1, 0, 2))
    sent = functools.partial(
        conv, rows, weight=conv_weight, decays=decays, lower=even,
        edge=jnp.where(is_even, is_bottom, is_top), sizes=sizes, dtype=BF16,
    )
    kept = functools.partial(
        conv, rows, weight=conv_weight, decays=decays, lower=odd,
        edge=jnp.where(is_even, is_top, is_bottom), sizes=sizes, dtype=F32,
    )
    early = 2
    *mine, top, bottom, token = sent(halos=[], start=0, count=early, after=[], edges=True)
    others = [lax.ppermute(value, "tm", swap) for value in mine]
    halos = [lax.ppermute(bottom, "space", down), lax.ppermute(top, "space", up)]
    *held, token = kept(halos=[], start=0, count=1, after=[token])
    *rest, token = sent(halos=halos, start=early, count=chunks - early, after=[token])
    others += [lax.ppermute(value, "tm", swap) for value in rest]
    coefs, token = coefficients(odd, decays, others[0], [token])

    lag = 3 * ((groups - 2) // 2) + 1
    drives, evens, odds, own, back = [], {}, {}, [], []
    drive, token = pair_drive(held[0], others[0], coefs, [token])
    drives.append(drive)
    for step in range(chunks + lag):
        ready = {
            g: drives[step - 3 * (g // 2)]
            for g in range(0, groups - 1, 2)
            if 0 <= step - 3 * (g // 2) < chunks
        }
        if ready:
            value, token = carry_on(group, coefs, ready, odds.get(step - 2), [token])
            evens[step] = lax.ppermute(value, "tm", even_hop)
        if step == 0:
            *more, token = kept(halos=halos, start=1, count=chunks - 1, after=[token])
            held += more
        if step + 1 < chunks:
            drive, token = pair_drive(held[step + 1], others[step + 1], coefs, [token])
            drives.append(drive)
        k = step - lag
        if k >= 0:
            carries = [
                evens[k + 3 * ((g - 1) // 2)] if g % 2 else odds[k + 1 + 3 * ((g - 2) // 2)]
                for g in range(1, groups)
            ]
            after = [token] + ([back[k - 2]] if k >= 2 else [])
            mine, theirs, token = states_of(group, coefs, held[k], others[k], carries, after)
            own.append(mine)
            back.append(lax.ppermute(theirs, "tm", swap))
        ready = {
            g: drives[step - 1 - 3 * ((g - 1) // 2)]
            for g in range(1, groups - 1, 2)
            if 0 <= step - 1 - 3 * ((g - 1) // 2) < chunks
        }
        if ready:
            value, token = carry_on(group, coefs, ready, evens[step - 1], [token])
            odds[step] = lax.ppermute(value, ("tm", "space"), odd_hop)

    skip = skip_gain[None]
    dtype = frames_in.dtype
    half_done, token = output_half(odd, rows, out_weight, skip, own, None, [token], dtype)
    result, token = output_half(even, rows, out_weight, skip, back, half_done, [token], dtype)
    return result[None]


def solution(mesh):
    placed = (P("tm", None, "space", None), P(), P(), P(), P("tm", None))
    return jax.shard_map(
        on_device,
        mesh=mesh,
        in_specs=placed,
        out_specs=P("tm", None, "space", None),
        check_vma=False,
    )
```

```python
import functools

import jax
import jax.numpy as jnp
from jax import lax
from jax.experimental import pallas as pl
from jax.experimental.pallas import tpu as pltpu
from jax.sharding import PartitionSpec as P

MIB = 1 << 20
VMEM = pl.BlockSpec(memory_space=pltpu.VMEM)
ANY = pl.BlockSpec(memory_space=pl.ANY)
SMEM = pl.BlockSpec(memory_space=pltpu.SMEM)
BF16, F32 = jnp.bfloat16, jnp.float32


def params(mib):
    return pltpu.CompilerParams(vmem_limit_bytes=mib * MIB)


def sizes_of(half):
    if half % 4 or half < 8:
        return [2] * (half // 2)
    return [2] + [4] * (half // 4 - 1) + [2]


def row(ref, q, channels):
    return ref[q * channels : (q + 1) * channels] if len(ref.shape) == 2 else ref[q]


PAD = 16
LANES = 128


def split_decays(decay):
    pieces = []
    rest = decay
    for _ in range(3):
        part = rest.astype(BF16).astype(F32)
        rest = rest - part
        pieces += [part[:, i : i + LANES] for i in range(0, decay.shape[1], LANES)]
    pieces += [jnp.zeros_like(pieces[0])] * (PAD - len(pieces))
    return jnp.concatenate(pieces, axis=0).astype(BF16)


def join_decays(block, count):
    block = block.astype(F32)
    n = count // LANES
    parts = [block[i : i + 1] + block[n + i : n + i + 1] + block[2 * n + i : 2 * n + i + 1] for i in range(n)]
    return jnp.concatenate(parts, axis=1)


def columns(*rows):
    rows = list(rows) + [rows[0]] * (8 - len(rows))
    return jnp.transpose(jnp.concatenate(rows, axis=0))


TOKEN = jax.ShapeDtypeStruct((8, 128), F32)


def call(kernel, out_shape, scalars, operands, after, name, mib=8, scratch=(), specs=None,
         out_specs=None, **more):
    specs = specs or [VMEM] * len(operands)
    out_specs = out_specs or [VMEM] * len(out_shape)
    n, outs = len(scalars) + len(operands), len(out_shape)

    def body(*refs):
        rest = refs[n + len(after) :]
        rest[outs][...] = jnp.zeros(TOKEN.shape, TOKEN.dtype)
        kernel(*refs[:n], *rest[:outs], *rest[outs + 1 :])

    return pl.pallas_call(
        body,
        out_shape=list(out_shape) + [TOKEN],
        in_specs=[SMEM] * len(scalars) + specs + [ANY] * len(after),
        out_specs=list(out_specs) + [VMEM],
        scratch_shapes=list(scratch),
        compiler_params=params(mib),
        cost_estimate=pl.CostEstimate(flops=1, bytes_accessed=1, transcendentals=0),
        name=name,
        **more,
    )(*scalars, *operands, *after)


def conv(rows_in, halos, weight, decays, lower, edge, sizes, start, count, dtype, after, edges=False, pair=None):
    tile_rows, channels, width = rows_in.shape
    states = weight.shape[2]
    half = tile_rows // 2
    mine = sizes[start : start + count]
    before, total = sum(sizes[:start]), sum(mine)
    whole = start + count == len(sizes)
    assert whole == bool(halos)
    out_shape = [jax.ShapeDtypeStruct((n, states, width), dtype) for n in mine]
    if pair:
        out_shape += [jax.ShapeDtypeStruct((n, states, width), dtype) for n in mine]
    if edges:
        out_shape += [jax.ShapeDtypeStruct((channels, width), rows_in.dtype)] * 2
        out_shape[0] = jax.ShapeDtypeStruct((mine[0] * states + PAD, width), dtype)

    def kernel(lower_ref, edge_ref, rows_ref, weight_ref, decays_ref, *refs):
        refs = list(refs)
        above, below = (refs.pop(0), refs.pop(0)) if whole else (None, None)
        other_ref, coefs_ref = (refs.pop(0), refs.pop(0)) if pair else (None, None)
        shifted, outs = refs.pop(), refs
        low = lower_ref[0]
        first_low, first_up = half + before - 1, half - before - total - 1
        first = first_up + low * (first_low - first_up)
        if edges:
            outs[count][...] = rows_ref[0]
            outs[count + 1][...] = rows_ref[tile_rows - 1]
            outs[0][mine[0] * states :] = split_decays(decays_ref[...])
        lane = lax.broadcasted_iota(jnp.int32, (channels, width), 1)

        def shift(n):
            slot = (total + 1 - n) + low * (2 * n - total - 1)
            if whole and n == total + 1:
                value = jnp.where(low == 1, below[...].astype(F32), above[...].astype(F32))
                value = jnp.where(edge_ref[0] == 1, 0.0, value)
            else:
                value = rows_ref[first + slot].astype(F32)
            left = jnp.where(lane == 0, 0.0, pltpu.roll(value, 1, 1))
            right = jnp.where(lane == width - 1, 0.0, pltpu.roll(value, width - 1, 1))
            shifted[slot, :channels] = left.astype(BF16)
            shifted[slot, channels : 2 * channels] = value.astype(BF16)
            shifted[slot, 2 * channels :] = right.astype(BF16)

        decay = decays_ref[...]
        gain = columns(jnp.sqrt(1.0 - decay * decay))[:, 0:1]
        taps = jnp.concatenate([weight_ref[i, j] for i in range(3) for j in range(3)], axis=1)
        for n in range(4):
            shift(n)
        done = 0
        for n, size in enumerate(mine):
            for q in range(0, size, 2):
                at = done + q
                r = (total - 2 - at) + low * (2 * at - total + 2)
                window = jnp.concatenate(
                    [
                        jnp.concatenate([shifted[r + i], shifted[r + i + 1]], axis=1)
                        for i in range(3)
                    ],
                    axis=0,
                )
                drive = gain * jnp.dot(taps, window, preferred_element_type=F32)
                place = (size - 2 - q) + low * (2 * q - size + 2)
                for i in range(2):
                    value = drive[:, i * width : (i + 1) * width].astype(dtype)
                    if len(outs[n].shape) == 2:
                        begin = pl.multiple_of((place + i) * states, states)
                        outs[n][pl.ds(begin, states)] = value
                    else:
                        outs[n][place + i] = value
                    if pair:
                        if len(other_ref.shape) == 2:
                            begin = pl.multiple_of((place + i) * states, states)
                            other = other_ref[pl.ds(begin, states)]
                        else:
                            other = other_ref[place + i]
                        outs[1][place + i] = (
                            coefs_ref[:, 1:2] * value + coefs_ref[:, 2:3] * other.astype(F32)
                        )
                for i in range(at + 4, min(at + 6, total + 2)):
                    shift(i)
            done += size

    return call(
        kernel, out_shape, [lower, edge],
        [rows_in, weight, decays] + list(halos) + list(pair or []), after, "conv_chunks", 14,
        scratch=[pltpu.VMEM((total + 2, 3 * channels, width), rows_in.dtype)],
    )


def coefficients(odd, own_decay, first, after):
    def kernel(odd_ref, own_ref, first_ref, out):
        is_odd = jnp.full(own_ref.shape, odd_ref[0], jnp.int32) == 1
        own = own_ref[...]
        other = join_decays(first_ref[first.shape[0] - PAD :], own.shape[1])
        both = own * other
        one, zero = jnp.ones_like(own), jnp.zeros_like(own)
        out[...] = columns(
            both,
            jnp.where(is_odd, one, other),
            jnp.where(is_odd, own, one),
            jnp.where(is_odd, both, own),
            jnp.where(is_odd, other, both),
            jnp.where(is_odd, own, zero),
            jnp.where(is_odd, zero, other),
        )

    shape = jax.ShapeDtypeStruct((own_decay.shape[1], 8), F32)
    return call(kernel, [shape], [odd], [own_decay, first], after, "coefficients")


def carry_on(group, coefs, drives, carry, after):
    groups = sorted(drives)
    most = max(drives[g].shape[0] for g in groups)
    shape = jax.ShapeDtypeStruct((most,) + drives[groups[0]].shape[1:], BF16)

    def kernel(group_ref, coefs_ref, *refs):
        out = refs[-1]
        out[...] = jnp.zeros_like(out)
        for g, ref in zip(groups, refs):

            @pl.when(group_ref[0] == g)
            def one(g=g, ref=ref):
                for q in range(ref.shape[0]):
                    total = ref[q]
                    if g > 0:
                        total = total + coefs_ref[:, 0:1] * refs[len(groups)][q].astype(F32)
                    out[q] = total.astype(BF16)

    operands = [coefs] + [drives[g] for g in groups] + ([carry] if carry is not None else [])
    return call(kernel, [shape], [group], operands, after, "carry_on")


def states_of(group, coefs, keep, other, carries, after):
    shape = jax.ShapeDtypeStruct(keep.shape, BF16)

    def kernel(group_ref, coefs_ref, keep_ref, other_ref, *refs):
        own, back = refs[-2:]

        def settle(carry_ref):
            for q in range(keep.shape[0]):
                held, sent = keep_ref[q], row(other_ref, q, keep.shape[1]).astype(F32)
                mine = held + coefs_ref[:, 5:6] * sent
                theirs = coefs_ref[:, 6:7] * held + sent
                if carry_ref is not None:
                    carry = carry_ref[q].astype(F32)
                    mine = mine + coefs_ref[:, 3:4] * carry
                    theirs = theirs + coefs_ref[:, 4:5] * carry
                own[q] = mine.astype(BF16)
                back[q] = theirs.astype(BF16)

        for g in range(len(carries) + 1):
            pl.when(group_ref[0] == g)(functools.partial(settle, refs[g - 1] if g else None))

    return call(
        kernel, [shape, shape], [group], [coefs, keep, other] + list(carries), after, "states_of"
    )


def output_half(lower, rows_in, weight, skip, states, earlier, after, dtype):
    tile_rows, channels, width = rows_in.shape
    half = tile_rows // 2
    pitch = channels + 1
    count = len(states)
    sizes = [value.shape[0] for value in states]

    def kernel(lower_ref, rows_ref, weight_ref, skip_ref, *refs):
        chunks = refs[:count]
        out, total, tile, sem = refs[-4:]
        low = lower_ref[0]
        begin = pl.multiple_of(low * half, half)
        gain = columns(skip_ref[...])[:, 0:1]
        done = 0
        for n, chunk in enumerate(chunks):
            at_up = half - done - sizes[n]
            r = at_up + low * (done - at_up)
            for q in range(0, sizes[n], 2):
                value = jnp.dot(
                    weight_ref[...],
                    jnp.concatenate([chunk[q], chunk[q + 1]], axis=1),
                    preferred_element_type=F32,
                )
                for i in range(2):
                    total[pl.ds((r + q + i) * pitch, channels), :] = value[
                        :, i * width : (i + 1) * width
                    ] + gain * rows_ref[begin + r + q + i].astype(F32)
            done += sizes[n]

        def settle(n, carry):
            for i in range(8):
                tile[n * 8 + i] = total[pl.ds(n * 8 + i, half, stride=pitch), :].astype(dtype)
            return carry

        lax.fori_loop(0, channels // 8, settle, 0, unroll=2)
        last = pltpu.make_async_copy(tile, out.at[:, pl.ds(begin, half), :], sem)
        last.start()
        last.wait()

    operands = [rows_in, weight, skip] + list(states)
    more = {}
    if earlier is not None:
        operands.append(earlier)
        more["input_output_aliases"] = {len(operands): 0}
    return call(
        kernel,
        [jax.ShapeDtypeStruct((channels, tile_rows, width), dtype)],
        [lower], operands, after, "output_half", 10,
        scratch=[
            pltpu.VMEM((half * pitch + 8, width), F32),
            pltpu.VMEM((channels, half, width), dtype),
            pltpu.SemaphoreType.DMA,
        ],
        specs=[VMEM] * (3 + count) + [ANY] * (len(operands) - 3 - count),
        out_specs=[ANY],
        **more,
    )


def on_device(frames_in, conv_weight, out_weight, skip_gain, decays):
    tile_rows = frames_in.shape[2]
    frames = lax.axis_size("tm")
    spaces = lax.axis_size("space")
    groups = frames // 2
    me, at = lax.axis_index("tm"), lax.axis_index("space")
    scalar = lambda value: jnp.asarray(value, jnp.int32).reshape(1)
    group, odd, even = scalar(me // 2), scalar(me % 2), scalar(1 - me % 2)
    is_top, is_bottom = scalar(at == 0), scalar(at == spaces - 1)
    is_even = me % 2 == 0
    sizes = sizes_of(tile_rows // 2)
    chunks = len(sizes)

    swap = [(i, i + 1 - 2 * (i % 2)) for i in range(frames)]
    even_hop = [(i, i + 2 if (i // 2) % 2 == 0 else i - 2) for i in range(frames)]
    odd_hop = [
        (i * spaces + j, i * spaces + j + 1 - 2 * (j % 2))
        if i // 2 in (0, groups - 1)
        else (i * spaces + j, (i + 2 if (i // 2) % 2 else i - 2) * spaces + j)
        for i in range(frames)
        for j in range(spaces)
    ]
    down = [(i, (i + 1) % spaces) for i in range(spaces)]
    up = [(i, (i - 1) % spaces) for i in range(spaces)]

    rows = jnp.transpose(frames_in[0], (1, 0, 2))
    sent = functools.partial(
        conv, rows, weight=conv_weight, decays=decays, lower=even,
        edge=jnp.where(is_even, is_bottom, is_top), sizes=sizes, dtype=BF16,
    )
    kept = functools.partial(
        conv, rows, weight=conv_weight, decays=decays, lower=odd,
        edge=jnp.where(is_even, is_top, is_bottom), sizes=sizes, dtype=F32,
    )
    early = 2
    *mine, top, bottom, token = sent(halos=[], start=0, count=early, after=[], edges=True)
    others = [lax.ppermute(value, "tm", swap) for value in mine]
    halos = [lax.ppermute(bottom, "space", down), lax.ppermute(top, "space", up)]
    coefs, token = coefficients(odd, decays, others[0], [token])
    held, drives = [], []

    def pair_drive(k, token):
        keep, drive, token = kept(
            halos=halos if k == chunks - 1 else [], start=k, count=1, after=[token],
            pair=[others[k], coefs],
        )
        held.append(keep)
        drives.append(drive)
        return token

    token = pair_drive(0, token)
    lag = 3 * ((groups - 2) // 2) + 1
    evens, odds, own, back = {}, {}, [], []
    early_pairs = [chunks - 1]
    waits = {("S", lag + 2): [0], ("E", lag + 3): [1], ("S", lag + chunks - 1): [chunks - 3]}

    def held_up(kind, step):
        return [back[n] for n in waits.get((kind, step), []) if 0 <= n < len(back)]

    for step in range(chunks + lag):
        ready = {
            g: drives[step - 3 * (g // 2)]
            for g in range(0, groups - 1, 2)
            if 0 <= step - 3 * (g // 2) < chunks
        }
        if ready:
            after = [token] + ([evens[0]] if step == 1 else []) + held_up('E', step)
            value, token = carry_on(group, coefs, ready, odds.get(step - 2), after)
            evens[step] = lax.ppermute(value, "tm", even_hop)
        if step == 0:
            *rest, token = sent(halos=halos, start=early, count=chunks - early, after=[token])
            others += [lax.ppermute(value, "tm", swap) for value in rest]
        k = step - lag
        if k >= 0:
            carries = [
                evens[k + 3 * ((g - 1) // 2)] if g % 2 else odds[k + 1 + 3 * ((g - 2) // 2)]
                for g in range(1, groups)
            ]
            after = [token] + held_up('S', step)
            mine, theirs, token = states_of(group, coefs, held[k], others[k], carries, after)
            own.append(mine)
            back.append(lax.ppermute(theirs, "tm", swap))
        if step + 1 in early_pairs:
            token = pair_drive(step + 1, token)
        ready = {
            g: drives[step - 1 - 3 * ((g - 1) // 2)]
            for g in range(1, groups - 1, 2)
            if 0 <= step - 1 - 3 * ((g - 1) // 2) < chunks
        }
        if ready:
            value, token = carry_on(group, coefs, ready, evens[step - 1], [token] + held_up('O', step))
            odds[step] = lax.ppermute(value, ("tm", "space"), odd_hop)
        if step + 1 < chunks and step + 1 not in early_pairs:
            token = pair_drive(step + 1, token)

    skip = skip_gain[None]
    dtype = frames_in.dtype
    half_done, token = output_half(odd, rows, out_weight, skip, own, None, [token], dtype)
    result, token = output_half(even, rows, out_weight, skip, back, half_done, [token], dtype)
    return result[None]


def solution(mesh):
    placed = (P("tm", None, "space", None), P(), P(), P(), P("tm", None))
    return jax.shard_map(
        on_device,
        mesh=mesh,
        in_specs=placed,
        out_specs=P("tm", None, "space", None),
        check_vma=False,
    )
```

```python
import functools

import jax
import jax.numpy as jnp
from jax import lax
from jax.experimental import pallas as pl
from jax.experimental.pallas import tpu as pltpu
from jax.sharding import PartitionSpec as P

MIB = 1 << 20
VMEM = pl.BlockSpec(memory_space=pltpu.VMEM)
ANY = pl.BlockSpec(memory_space=pl.ANY)
SMEM = pl.BlockSpec(memory_space=pltpu.SMEM)
BF16, F32 = jnp.bfloat16, jnp.float32


def params(mib):
    return pltpu.CompilerParams(vmem_limit_bytes=mib * MIB)


def sizes_of(half):
    if half % 4 or half < 8:
        return [2] * (half // 2)
    return [2] + [4] * (half // 4 - 1) + [2]


PAD = 16
LANES = 128


def split_decays(decay):
    pieces = []
    rest = decay
    for _ in range(3):
        part = rest.astype(BF16).astype(F32)
        rest = rest - part
        pieces += [part[:, i : i + LANES] for i in range(0, decay.shape[1], LANES)]
    pieces += [jnp.zeros_like(pieces[0])] * (PAD - len(pieces))
    return jnp.concatenate(pieces, axis=0).astype(BF16)


def join_decays(block, count):
    block = block.astype(F32)
    n = count // LANES
    parts = [block[i : i + 1] + block[n + i : n + i + 1] + block[2 * n + i : 2 * n + i + 1] for i in range(n)]
    return jnp.concatenate(parts, axis=1)


def columns(*rows):
    rows = list(rows) + [rows[0]] * (8 - len(rows))
    return jnp.transpose(jnp.concatenate(rows, axis=0))


TOKEN = jax.ShapeDtypeStruct((8, 128), F32)


def call(kernel, out_shape, scalars, operands, after, name, mib=8, scratch=(), specs=None,
         out_specs=None, **more):
    specs = specs or [VMEM] * len(operands)
    out_specs = out_specs or [VMEM] * len(out_shape)
    n, outs = len(scalars) + len(operands), len(out_shape)

    def body(*refs):
        rest = refs[n + len(after) :]
        rest[outs][...] = jnp.zeros(TOKEN.shape, TOKEN.dtype)
        kernel(*refs[:n], *rest[:outs], *rest[outs + 1 :])

    return pl.pallas_call(
        body,
        out_shape=list(out_shape) + [TOKEN],
        in_specs=[SMEM] * len(scalars) + specs + [ANY] * len(after),
        out_specs=list(out_specs) + [VMEM],
        scratch_shapes=list(scratch),
        compiler_params=params(mib),
        cost_estimate=pl.CostEstimate(flops=1, bytes_accessed=1, transcendentals=0),
        name=name,
        **more,
    )(*scalars, *operands, *after)


def conv(rows_in, halos, weight, decays, lower, edge, sizes, start, count, dtype, after, edges=False, pair=None):
    tile_rows, channels, width = rows_in.shape
    states = weight.shape[2]
    half = tile_rows // 2
    mine = sizes[start : start + count]
    before, total = sum(sizes[:start]), sum(mine)
    whole = start + count == len(sizes)
    assert whole == bool(halos)
    out_shape = [jax.ShapeDtypeStruct((n, states, width), dtype) for n in mine]
    if pair:
        out_shape += [jax.ShapeDtypeStruct((n, states, width), dtype) for n in mine]
    if edges:
        out_shape += [jax.ShapeDtypeStruct((channels, width), rows_in.dtype)] * 2
        out_shape[0] = jax.ShapeDtypeStruct((mine[0] * states + PAD, width), dtype)

    def kernel(lower_ref, edge_ref, rows_ref, weight_ref, decays_ref, *refs):
        refs = list(refs)
        above, below = (refs.pop(0), refs.pop(0)) if whole else (None, None)
        other_ref, coefs_ref = (refs.pop(0), refs.pop(0)) if pair else (None, None)
        shifted, outs = refs.pop(), refs
        low = lower_ref[0]
        first_low, first_up = half + before - 1, half - before - total - 1
        first = first_up + low * (first_low - first_up)
        if edges:
            outs[count][...] = rows_ref[0]
            outs[count + 1][...] = rows_ref[tile_rows - 1]
            outs[0][mine[0] * states :] = split_decays(decays_ref[...])
        lane = lax.broadcasted_iota(jnp.int32, (channels, width), 1)

        def shift(n):
            slot = (total + 1 - n) + low * (2 * n - total - 1)
            if whole and n == total + 1:
                value = jnp.where(low == 1, below[...].astype(F32), above[...].astype(F32))
                value = jnp.where(edge_ref[0] == 1, 0.0, value)
            else:
                value = rows_ref[first + slot].astype(F32)
            left = jnp.where(lane == 0, 0.0, pltpu.roll(value, 1, 1))
            right = jnp.where(lane == width - 1, 0.0, pltpu.roll(value, width - 1, 1))
            shifted[slot, :channels] = left.astype(BF16)
            shifted[slot, channels : 2 * channels] = value.astype(BF16)
            shifted[slot, 2 * channels :] = right.astype(BF16)

        decay = decays_ref[...]
        gain = columns(jnp.sqrt(1.0 - decay * decay))[:, 0:1]
        taps = jnp.concatenate([weight_ref[i, j] for i in range(3) for j in range(3)], axis=1)
        for n in range(4):
            shift(n)
        done = 0
        for n, size in enumerate(mine):
            for q in range(0, size, 2):
                at = done + q
                r = (total - 2 - at) + low * (2 * at - total + 2)
                window = jnp.concatenate(
                    [
                        jnp.concatenate([shifted[r + i], shifted[r + i + 1]], axis=1)
                        for i in range(3)
                    ],
                    axis=0,
                )
                drive = gain * jnp.dot(taps, window, preferred_element_type=F32)
                place = (size - 2 - q) + low * (2 * q - size + 2)
                for i in range(2):
                    value = drive[:, i * width : (i + 1) * width].astype(dtype)
                    begin = pl.multiple_of((place + i) * states, states)
                    if pair:
                        flat = len(other_ref.shape) == 2
                        other = other_ref[pl.ds(begin, states) if flat else place + i].astype(F32)
                        outs[0][place + i] = jnp.where(low == 1, other, value)
                        outs[1][place + i] = (
                            coefs_ref[:, 1:2] * value + coefs_ref[:, 2:3] * other
                        )
                    elif len(outs[n].shape) == 2:
                        outs[n][pl.ds(begin, states)] = value
                    else:
                        outs[n][place + i] = value
                for i in range(at + 4, min(at + 6, total + 2)):
                    shift(i)
            done += size

    return call(
        kernel, out_shape, [lower, edge],
        [rows_in, weight, decays] + list(halos) + list(pair or []), after, "conv_chunks", 14,
        scratch=[pltpu.VMEM((total + 2, 3 * channels, width), rows_in.dtype)],
    )


def coefficients(odd, own_decay, first, after):
    def kernel(odd_ref, own_ref, first_ref, out):
        is_odd = jnp.full(own_ref.shape, odd_ref[0], jnp.int32) == 1
        own = own_ref[...]
        other = join_decays(first_ref[first.shape[0] - PAD :], own.shape[1])
        both = own * other
        one = jnp.ones_like(own)
        out[...] = columns(
            both,
            jnp.where(is_odd, one, other),
            jnp.where(is_odd, own, one),
            jnp.where(is_odd, other, own),
        )

    shape = jax.ShapeDtypeStruct((own_decay.shape[1], 8), F32)
    return call(kernel, [shape], [odd], [own_decay, first], after, "coefficients")


def carry_on(group, coefs, drives, carry, after):
    groups = sorted(drives)
    most = max(drives[g].shape[0] for g in groups)
    shape = jax.ShapeDtypeStruct((most,) + drives[groups[0]].shape[1:], BF16)

    def kernel(group_ref, coefs_ref, *refs):
        out = refs[-1]
        out[...] = jnp.zeros_like(out)
        for g, ref in zip(groups, refs):

            @pl.when(group_ref[0] == g)
            def one(g=g, ref=ref):
                for q in range(ref.shape[0]):
                    total = ref[q]
                    if g > 0:
                        total = total + coefs_ref[:, 0:1] * refs[len(groups)][q].astype(F32)
                    out[q] = total.astype(BF16)

    operands = [coefs] + [drives[g] for g in groups] + ([carry] if carry is not None else [])
    return call(kernel, [shape], [group], operands, after, "carry_on")


def states_of(group, odd, coefs, first, pair, carries, after):
    shape = jax.ShapeDtypeStruct(first.shape, BF16)

    def kernel(group_ref, odd_ref, coefs_ref, first_ref, pair_ref, *refs):
        own, back = refs[-2:]

        def settle(carry_ref, of_even, of_odd):
            for q in range(first.shape[0]):
                even_state, odd_state = first_ref[q], pair_ref[q]
                if carry_ref is not None:
                    carry = carry_ref[q].astype(F32)
                    even_state = even_state + coefs_ref[:, 3:4] * carry
                    odd_state = odd_state + coefs_ref[:, 0:1] * carry
                of_even[q] = even_state.astype(BF16)
                of_odd[q] = odd_state.astype(BF16)

        for g in range(len(carries) + 1):
            carry_ref = refs[g - 1] if g else None
            here = group_ref[0] == g
            pl.when(here & (odd_ref[0] == 0))(functools.partial(settle, carry_ref, own, back))
            pl.when(here & (odd_ref[0] == 1))(functools.partial(settle, carry_ref, back, own))

    operands = [coefs, first, pair] + list(carries)
    return call(kernel, [shape, shape], [group, odd], operands, after, "states_of")


def output_half(lower, rows_in, weight, skip, states, earlier, after, dtype):
    tile_rows, channels, width = rows_in.shape
    half = tile_rows // 2
    pitch = channels + 1
    count = len(states)
    sizes = [value.shape[0] for value in states]
    blocks = 4 if channels % 64 == 0 else 1

    def kernel(lower_ref, rows_ref, weight_ref, skip_ref, *refs):
        chunks = refs[:count]
        out, total, tile, sems = refs[-4:]
        low = lower_ref[0]
        begin = pl.multiple_of(low * half, half)
        gain = columns(skip_ref[...])[:, 0:1]
        done = 0
        for n, chunk in enumerate(chunks):
            at_up = half - done - sizes[n]
            r = at_up + low * (done - at_up)
            for q in range(0, sizes[n], 2):
                value = jnp.dot(
                    weight_ref[...],
                    jnp.concatenate([chunk[q], chunk[q + 1]], axis=1),
                    preferred_element_type=F32,
                )
                for i in range(2):
                    total[pl.ds((r + q + i) * pitch, channels), :] = value[
                        :, i * width : (i + 1) * width
                    ] + gain * rows_ref[begin + r + q + i].astype(F32)
            done += sizes[n]

        def settle(n, carry):
            for i in range(8):
                tile[n * 8 + i] = total[pl.ds(n * 8 + i, half, stride=pitch), :].astype(dtype)
            return carry

        copies = []
        size = channels // blocks
        for n in range(blocks):
            lax.fori_loop(n * size // 8, (n + 1) * size // 8, settle, 0, unroll=2)
            part = pl.ds(n * size, size)
            copies.append(
                pltpu.make_async_copy(
                    tile.at[part], out.at[part, pl.ds(begin, half), :], sems.at[n]
                )
            )
            copies[-1].start()
        for copy in copies:
            copy.wait()

    operands = [rows_in, weight, skip] + list(states)
    more = {}
    if earlier is not None:
        operands.append(earlier)
        more["input_output_aliases"] = {len(operands): 0}
    return call(
        kernel,
        [jax.ShapeDtypeStruct((channels, tile_rows, width), dtype)],
        [lower], operands, after, "output_half", 10,
        scratch=[
            pltpu.VMEM(((half + 1) * pitch + 7, width), F32),
            pltpu.VMEM((channels, half, width), dtype),
            pltpu.SemaphoreType.DMA((blocks,)),
        ],
        specs=[VMEM] * (3 + count) + [ANY] * (len(operands) - 3 - count),
        out_specs=[ANY],
        **more,
    )


def on_device(frames_in, conv_weight, out_weight, skip_gain, decays):
    tile_rows = frames_in.shape[2]
    frames = lax.axis_size("tm")
    spaces = lax.axis_size("space")
    groups = frames // 2
    me, at = lax.axis_index("tm"), lax.axis_index("space")
    scalar = lambda value: jnp.asarray(value, jnp.int32).reshape(1)
    group, odd, even = scalar(me // 2), scalar(me % 2), scalar(1 - me % 2)
    is_top, is_bottom = scalar(at == 0), scalar(at == spaces - 1)
    is_even = me % 2 == 0
    sizes = sizes_of(tile_rows // 2)
    chunks = len(sizes)

    swap = [(i, i + 1 - 2 * (i % 2)) for i in range(frames)]
    even_hop = [(i, i + 2 if (i // 2) % 2 == 0 else i - 2) for i in range(frames)]
    odd_hop = [
        (i * spaces + j, i * spaces + j + 1 - 2 * (j % 2))
        if i // 2 in (0, groups - 1)
        else (i * spaces + j, (i + 2 if (i // 2) % 2 else i - 2) * spaces + j)
        for i in range(frames)
        for j in range(spaces)
    ]
    down = [(i, (i + 1) % spaces) for i in range(spaces)]
    up = [(i, (i - 1) % spaces) for i in range(spaces)]

    rows = jnp.transpose(frames_in[0], (1, 0, 2))
    sent = functools.partial(
        conv, rows, weight=conv_weight, decays=decays, lower=even,
        edge=jnp.where(is_even, is_bottom, is_top), sizes=sizes, dtype=BF16,
    )
    kept = functools.partial(
        conv, rows, weight=conv_weight, decays=decays, lower=odd,
        edge=jnp.where(is_even, is_top, is_bottom), sizes=sizes, dtype=F32,
    )
    early = 2
    *mine, top, bottom, token = sent(halos=[], start=0, count=early, after=[], edges=True)
    others = [lax.ppermute(value, "tm", swap) for value in mine]
    halos = [lax.ppermute(bottom, "space", down), lax.ppermute(top, "space", up)]
    coefs, token = coefficients(odd, decays, others[0], [token])
    held, drives = [], []

    def pair_drive(k, token, after=[]):
        keep, drive, token = kept(
            halos=halos if k == chunks - 1 else [], start=k, count=1, after=[token] + after,
            pair=[others[k], coefs],
        )
        held.append(keep)
        drives.append(drive)
        return token

    token = pair_drive(0, token)
    lag = 3 * ((groups - 2) // 2) + 1
    evens, odds, own, back = {}, {}, [], []
    waits = {('O', lag + 1): [0], ('E', lag + 3): [1], ('S', lag + chunks - 1): [chunks - 3]}

    def held_up(kind, step):
        return [back[n] for n in waits.get((kind, step), []) if 0 <= n < len(back)]

    for step in range(chunks + lag):
        ready = {
            g: drives[step - 3 * (g // 2)]
            for g in range(0, groups - 1, 2)
            if 0 <= step - 3 * (g // 2) < chunks
        }
        if ready:
            after = [token] + [] + held_up('E', step)
            value, token = carry_on(group, coefs, ready, odds.get(step - 2), after)
            evens[step] = lax.ppermute(value, "tm", even_hop)
        if step == 0:
            *rest, token = sent(halos=halos, start=early, count=chunks - early, after=[token])
            others += [lax.ppermute(value, "tm", swap) for value in rest]
        k = step - lag
        if k >= 0:
            carries = [
                evens[k + 3 * ((g - 1) // 2)] if g % 2 else odds[k + 1 + 3 * ((g - 2) // 2)]
                for g in range(1, groups)
            ]
            after = [token] + held_up('S', step)
            mine, theirs, token = states_of(group, odd, coefs, held[k], drives[k], carries, after)
            own.append(mine)
            back.append(lax.ppermute(theirs, "tm", swap))
        ready = {
            g: drives[step - 1 - 3 * ((g - 1) // 2)]
            for g in range(1, groups - 1, 2)
            if 0 <= step - 1 - 3 * ((g - 1) // 2) < chunks
        }
        if ready:
            value, token = carry_on(group, coefs, ready, evens[step - 1], [token] + held_up('O', step))
            odds[step] = lax.ppermute(value, ("tm", "space"), odd_hop)
        if step + 1 < chunks:
            token = pair_drive(step + 1, token, [evens[0]] if step == 0 else [])

    skip = skip_gain[None]
    dtype = frames_in.dtype
    half_done, token = output_half(odd, rows, out_weight, skip, own, None, [token], dtype)
    result, token = output_half(even, rows, out_weight, skip, back, half_done, [token], dtype)
    return result[None]


def solution(mesh):
    placed = (P("tm", None, "space", None), P(), P(), P(), P("tm", None))
    return jax.shard_map(
        on_device,
        mesh=mesh,
        in_specs=placed,
        out_specs=P("tm", None, "space", None),
        check_vma=False,
    )
```

```python
import functools

import jax
import jax.numpy as jnp
from jax import lax
from jax.experimental import pallas as pl
from jax.experimental.pallas import tpu as pltpu
from jax.sharding import PartitionSpec as P

MIB = 1 << 20
VMEM = pl.BlockSpec(memory_space=pltpu.VMEM)
ANY = pl.BlockSpec(memory_space=pl.ANY)
SMEM = pl.BlockSpec(memory_space=pltpu.SMEM)
BF16, F32 = jnp.bfloat16, jnp.float32


def params(mib):
    return pltpu.CompilerParams(vmem_limit_bytes=mib * MIB)


def sizes_of(half):
    if half % 4 or half < 8:
        return [2] * (half // 2)
    return [2] + [4] * (half // 4 - 1) + [2]


PAD = 16
LANES = 128


def split_decays(decay):
    pieces = []
    rest = decay
    for _ in range(3):
        part = rest.astype(BF16).astype(F32)
        rest = rest - part
        pieces += [part[:, i : i + LANES] for i in range(0, decay.shape[1], LANES)]
    pieces += [jnp.zeros_like(pieces[0])] * (PAD - len(pieces))
    return jnp.concatenate(pieces, axis=0).astype(BF16)


def join_decays(block, count):
    block = block.astype(F32)
    n = count // LANES
    parts = [block[i : i + 1] + block[n + i : n + i + 1] + block[2 * n + i : 2 * n + i + 1] for i in range(n)]
    return jnp.concatenate(parts, axis=1)


def columns(*rows):
    rows = list(rows) + [rows[0]] * (8 - len(rows))
    return jnp.transpose(jnp.concatenate(rows, axis=0))


TOKEN = jax.ShapeDtypeStruct((8, 128), F32)


def call(kernel, out_shape, scalars, operands, after, name, mib=8, scratch=(), specs=None,
         out_specs=None, **more):
    specs = specs or [VMEM] * len(operands)
    out_specs = out_specs or [VMEM] * len(out_shape)
    n, outs = len(scalars) + len(operands), len(out_shape)

    def body(*refs):
        rest = refs[n + len(after) :]
        rest[outs][...] = jnp.zeros(TOKEN.shape, TOKEN.dtype)
        kernel(*refs[:n], *rest[:outs], *rest[outs + 1 :])

    return pl.pallas_call(
        body,
        out_shape=list(out_shape) + [TOKEN],
        in_specs=[SMEM] * len(scalars) + specs + [ANY] * len(after),
        out_specs=list(out_specs) + [VMEM],
        scratch_shapes=list(scratch),
        compiler_params=params(mib),
        cost_estimate=pl.CostEstimate(flops=1, bytes_accessed=1, transcendentals=0),
        name=name,
        **more,
    )(*scalars, *operands, *after)


def conv(rows_in, halos, weight, decays, lower, edge, sizes, start, count, dtype, after, edges=False, pair=None):
    tile_rows, channels, width = rows_in.shape
    states = weight.shape[2]
    half = tile_rows // 2
    mine = sizes[start : start + count]
    before, total = sum(sizes[:start]), sum(mine)
    whole = start + count == len(sizes)
    assert whole == bool(halos)
    out_shape = [jax.ShapeDtypeStruct((n, states, width), dtype) for n in mine]
    if pair:
        out_shape += [jax.ShapeDtypeStruct((n, states, width), dtype) for n in mine]
    if edges:
        out_shape += [jax.ShapeDtypeStruct((channels, width), rows_in.dtype)] * 2
        out_shape[0] = jax.ShapeDtypeStruct((mine[0] * states + PAD, width), dtype)

    def kernel(lower_ref, edge_ref, rows_ref, weight_ref, decays_ref, *refs):
        refs = list(refs)
        above, below = (refs.pop(0), refs.pop(0)) if whole else (None, None)
        other_ref, coefs_ref = (refs.pop(0), refs.pop(0)) if pair else (None, None)
        shifted, outs = refs.pop(), refs
        low = lower_ref[0]
        first_low, first_up = half + before - 1, half - before - total - 1
        first = first_up + low * (first_low - first_up)
        if edges:
            outs[count][...] = rows_ref[0]
            outs[count + 1][...] = rows_ref[tile_rows - 1]
            outs[0][mine[0] * states :] = split_decays(decays_ref[...])
        lane = lax.broadcasted_iota(jnp.int32, (channels, width), 1)

        def shift(n):
            slot = (total + 1 - n) + low * (2 * n - total - 1)
            if whole and n == total + 1:
                value = jnp.where(low == 1, below[...].astype(F32), above[...].astype(F32))
                value = jnp.where(edge_ref[0] == 1, 0.0, value)
            else:
                value = rows_ref[first + slot].astype(F32)
            left = jnp.where(lane == 0, 0.0, pltpu.roll(value, 1, 1))
            right = jnp.where(lane == width - 1, 0.0, pltpu.roll(value, width - 1, 1))
            shifted[slot, :channels] = left.astype(BF16)
            shifted[slot, channels : 2 * channels] = value.astype(BF16)
            shifted[slot, 2 * channels :] = right.astype(BF16)

        decay = decays_ref[...]
        gain = columns(jnp.sqrt(1.0 - decay * decay))[:, 0:1]
        taps = jnp.concatenate([weight_ref[i, j] for i in range(3) for j in range(3)], axis=1)
        for n in range(4):
            shift(n)
        done = 0
        for n, size in enumerate(mine):
            for q in range(0, size, 2):
                at = done + q
                r = (total - 2 - at) + low * (2 * at - total + 2)
                window = jnp.concatenate(
                    [
                        jnp.concatenate([shifted[r + i], shifted[r + i + 1]], axis=1)
                        for i in range(3)
                    ],
                    axis=0,
                )
                drive = gain * jnp.dot(taps, window, preferred_element_type=F32)
                place = (size - 2 - q) + low * (2 * q - size + 2)
                for i in range(2):
                    value = drive[:, i * width : (i + 1) * width].astype(dtype)
                    begin = pl.multiple_of((place + i) * states, states)
                    if pair:
                        flat = len(other_ref.shape) == 2
                        other = other_ref[pl.ds(begin, states) if flat else place + i].astype(F32)
                        outs[0][place + i] = jnp.where(low == 1, other, value)
                        outs[1][place + i] = (
                            coefs_ref[:, 1:2] * value + coefs_ref[:, 2:3] * other
                        )
                    elif len(outs[n].shape) == 2:
                        outs[n][pl.ds(begin, states)] = value
                    else:
                        outs[n][place + i] = value
                for i in range(at + 4, min(at + 6, total + 2)):
                    shift(i)
            done += size

    return call(
        kernel, out_shape, [lower, edge],
        [rows_in, weight, decays] + list(halos) + list(pair or []), after, "conv_chunks", 14,
        scratch=[pltpu.VMEM((total + 2, 3 * channels, width), rows_in.dtype)],
    )


def coefficients(odd, own_decay, first, after):
    def kernel(odd_ref, own_ref, first_ref, out):
        is_odd = jnp.full(own_ref.shape, odd_ref[0], jnp.int32) == 1
        own = own_ref[...]
        other = join_decays(first_ref[first.shape[0] - PAD :], own.shape[1])
        both = own * other
        one = jnp.ones_like(own)
        out[...] = columns(
            both,
            jnp.where(is_odd, one, other),
            jnp.where(is_odd, own, one),
            jnp.where(is_odd, other, own),
        )

    shape = jax.ShapeDtypeStruct((own_decay.shape[1], 8), F32)
    return call(kernel, [shape], [odd], [own_decay, first], after, "coefficients")


def carry_on(group, coefs, drives, carry, after):
    groups = sorted(drives)
    most = max(drives[g].shape[0] for g in groups)
    shape = jax.ShapeDtypeStruct((most,) + drives[groups[0]].shape[1:], BF16)

    def kernel(group_ref, coefs_ref, *refs):
        out = refs[-1]
        out[...] = jnp.zeros_like(out)
        for g, ref in zip(groups, refs):

            @pl.when(group_ref[0] == g)
            def one(g=g, ref=ref):
                for q in range(ref.shape[0]):
                    total = ref[q]
                    if g > 0:
                        total = total + coefs_ref[:, 0:1] * refs[len(groups)][q].astype(F32)
                    out[q] = total.astype(BF16)

    operands = [coefs] + [drives[g] for g in groups] + ([carry] if carry is not None else [])
    return call(kernel, [shape], [group], operands, after, "carry_on")


def states_of(group, odd, coefs, first, pair, carries, after):
    shape = jax.ShapeDtypeStruct(first.shape, BF16)

    def kernel(group_ref, odd_ref, coefs_ref, first_ref, pair_ref, *refs):
        own, back = refs[-2:]

        def settle(carry_ref, of_even, of_odd):
            for q in range(first.shape[0]):
                even_state, odd_state = first_ref[q], pair_ref[q]
                if carry_ref is not None:
                    carry = carry_ref[q].astype(F32)
                    even_state = even_state + coefs_ref[:, 3:4] * carry
                    odd_state = odd_state + coefs_ref[:, 0:1] * carry
                of_even[q] = even_state.astype(BF16)
                of_odd[q] = odd_state.astype(BF16)

        for g in range(len(carries) + 1):
            carry_ref = refs[g - 1] if g else None
            here = group_ref[0] == g
            pl.when(here & (odd_ref[0] == 0))(functools.partial(settle, carry_ref, own, back))
            pl.when(here & (odd_ref[0] == 1))(functools.partial(settle, carry_ref, back, own))

    operands = [coefs, first, pair] + list(carries)
    return call(kernel, [shape, shape], [group, odd], operands, after, "states_of")


def output_half(lower, rows_in, weight, skip, states, begun, earlier, after, dtype, finish=True):
    tile_rows, channels, width = rows_in.shape
    half = tile_rows // 2
    pitch = channels + 1
    sizes = sizes_of(half)
    here = [n for n, value in enumerate(states) if value is not None]
    count = len(here)
    blocks = 4 if channels % 64 == 0 else 1
    held_rows = (half + 1) * pitch + 7

    def kernel(lower_ref, rows_ref, weight_ref, skip_ref, *refs):
        chunks = dict(zip(here, refs[:count]))
        if finish:
            total, tile, sems = refs[-3:]
            out = refs[-4]
        else:
            total = refs[-1]
        low = lower_ref[0]
        begin = pl.multiple_of(low * half, half)
        gain = columns(skip_ref[...])[:, 0:1]
        for n, chunk in chunks.items():
            done = sum(sizes[:n])
            at_up = half - done - sizes[n]
            r = at_up + low * (done - at_up)
            for q in range(0, sizes[n], 2):
                value = jnp.dot(
                    weight_ref[...],
                    jnp.concatenate([chunk[q], chunk[q + 1]], axis=1),
                    preferred_element_type=F32,
                )
                for i in range(2):
                    total[pl.ds((r + q + i) * pitch, channels), :] = value[
                        :, i * width : (i + 1) * width
                    ] + gain * rows_ref[begin + r + q + i].astype(F32)
        if not finish:
            return
        if begun is not None:
            begun_ref = refs[count]
            now = [sum(sizes[: here[0]]), sum(sizes[: here[-1] + 1])]
            low_at = [half - now[1], half - now[0]]
            first = low_at[0] + low * (now[0] - low_at[0])
            last_row = low_at[1] + low * (now[1] - low_at[1])
            at = lax.broadcasted_iota(jnp.int32, (half, width), 0)
            fresh = (at >= first) & (at < last_row)

        def settle(n, carry):
            for i in range(8):
                value = total[pl.ds(n * 8 + i, half, stride=pitch), :]
                if begun is not None:
                    old = begun_ref[pl.ds(n * 8 + i, half, stride=pitch), :]
                    value = jnp.where(fresh, value, old)
                tile[n * 8 + i] = value.astype(dtype)
            return carry

        copies = []
        size = channels // blocks
        for n in range(blocks):
            lax.fori_loop(n * size // 8, (n + 1) * size // 8, settle, 0, unroll=2)
            part = pl.ds(n * size, size)
            copies.append(
                pltpu.make_async_copy(
                    tile.at[part], out.at[part, pl.ds(begin, half), :], sems.at[n]
                )
            )
            copies[-1].start()
        for copy in copies:
            copy.wait()

    operands = [rows_in, weight, skip] + [states[n] for n in here]
    if begun is not None:
        operands.append(begun)
    in_place = len(operands)
    more = {}
    if earlier is not None:
        operands.append(earlier)
        more["input_output_aliases"] = {len(operands): 0}
    specs = [VMEM] * in_place + [ANY] * (len(operands) - in_place)
    if not finish:
        shape = jax.ShapeDtypeStruct((held_rows, width), F32)
        return call(kernel, [shape], [lower], operands, after, "output_begun", 10, specs=specs)
    return call(
        kernel,
        [jax.ShapeDtypeStruct((channels, tile_rows, width), dtype)],
        [lower], operands, after, "output_half", 10,
        scratch=[
            pltpu.VMEM((held_rows, width), F32),
            pltpu.VMEM((channels, half, width), dtype),
            pltpu.SemaphoreType.DMA((blocks,)),
        ],
        specs=specs,
        out_specs=[ANY],
        **more,
    )


def on_device(frames_in, conv_weight, out_weight, skip_gain, decays):
    tile_rows = frames_in.shape[2]
    frames = lax.axis_size("tm")
    spaces = lax.axis_size("space")
    groups = frames // 2
    me, at = lax.axis_index("tm"), lax.axis_index("space")
    scalar = lambda value: jnp.asarray(value, jnp.int32).reshape(1)
    group, odd, even = scalar(me // 2), scalar(me % 2), scalar(1 - me % 2)
    is_top, is_bottom = scalar(at == 0), scalar(at == spaces - 1)
    is_even = me % 2 == 0
    sizes = sizes_of(tile_rows // 2)
    chunks = len(sizes)

    swap = [(i, i + 1 - 2 * (i % 2)) for i in range(frames)]
    even_hop = [(i, i + 2 if (i // 2) % 2 == 0 else i - 2) for i in range(frames)]
    odd_hop = [
        (i * spaces + j, i * spaces + j + 1 - 2 * (j % 2))
        if i // 2 in (0, groups - 1)
        else (i * spaces + j, (i + 2 if (i // 2) % 2 else i - 2) * spaces + j)
        for i in range(frames)
        for j in range(spaces)
    ]
    down = [(i, (i + 1) % spaces) for i in range(spaces)]
    up = [(i, (i - 1) % spaces) for i in range(spaces)]

    rows = jnp.transpose(frames_in[0], (1, 0, 2))
    sent = functools.partial(
        conv, rows, weight=conv_weight, decays=decays, lower=even,
        edge=jnp.where(is_even, is_bottom, is_top), sizes=sizes, dtype=BF16,
    )
    kept = functools.partial(
        conv, rows, weight=conv_weight, decays=decays, lower=odd,
        edge=jnp.where(is_even, is_top, is_bottom), sizes=sizes, dtype=F32,
    )
    early = 2
    *mine, top, bottom, token = sent(halos=[], start=0, count=early, after=[], edges=True)
    others = [lax.ppermute(value, "tm", swap) for value in mine]
    halos = [lax.ppermute(bottom, "space", down), lax.ppermute(top, "space", up)]
    coefs, token = coefficients(odd, decays, others[0], [token])
    held, drives = [], []

    def pair_drive(k, token, after=[]):
        keep, drive, token = kept(
            halos=halos if k == chunks - 1 else [], start=k, count=1, after=[token] + after,
            pair=[others[k], coefs],
        )
        held.append(keep)
        drives.append(drive)
        return token

    token = pair_drive(0, token)
    lag = 3 * ((groups - 2) // 2) + 1
    evens, odds, own, back = {}, {}, [], []
    waits = {('O', lag + 1): [0], ('E', lag + 3): [1], ('S', lag + chunks - 1): [chunks - 3]}

    def held_up(kind, step):
        return [back[n] for n in waits.get((kind, step), []) if 0 <= n < len(back)]

    for step in range(chunks + lag):
        ready = {
            g: drives[step - 3 * (g // 2)]
            for g in range(0, groups - 1, 2)
            if 0 <= step - 3 * (g // 2) < chunks
        }
        if ready:
            after = [token] + [] + held_up('E', step)
            value, token = carry_on(group, coefs, ready, odds.get(step - 2), after)
            evens[step] = lax.ppermute(value, "tm", even_hop)
        if step == 0:
            *rest, token = sent(halos=halos, start=early, count=chunks - early, after=[token])
            others += [lax.ppermute(value, "tm", swap) for value in rest]
        k = step - lag
        if k >= 0:
            carries = [
                evens[k + 3 * ((g - 1) // 2)] if g % 2 else odds[k + 1 + 3 * ((g - 2) // 2)]
                for g in range(1, groups)
            ]
            after = [token] + held_up('S', step)
            mine, theirs, token = states_of(group, odd, coefs, held[k], drives[k], carries, after)
            own.append(mine)
            back.append(lax.ppermute(theirs, "tm", swap))
        ready = {
            g: drives[step - 1 - 3 * ((g - 1) // 2)]
            for g in range(1, groups - 1, 2)
            if 0 <= step - 1 - 3 * ((g - 1) // 2) < chunks
        }
        if ready:
            value, token = carry_on(group, coefs, ready, evens[step - 1], [token] + held_up('O', step))
            odds[step] = lax.ppermute(value, ("tm", "space"), odd_hop)
        if step + 1 < chunks:
            token = pair_drive(step + 1, token, [evens[0]] if step == 0 else [])

    skip = skip_gain[None]
    dtype = frames_in.dtype
    half_done, token = output_half(
        odd, rows, out_weight, skip, own, None, None, [token], dtype
    )
    begun, token = output_half(
        even, rows, out_weight, skip, back[:-2] + [None] * 2, None, None, [token], dtype, finish=False
    )
    result, token = output_half(
        even, rows, out_weight, skip, [None] * (chunks - 2) + back[-2:], begun, half_done,
        [token], dtype,
    )
    return result[None]


def solution(mesh):
    placed = (P("tm", None, "space", None), P(), P(), P(), P("tm", None))
    return jax.shard_map(
        on_device,
        mesh=mesh,
        in_specs=placed,
        out_specs=P("tm", None, "space", None),
        check_vma=False,
    )
```

```python
import functools

import jax
import jax.numpy as jnp
from jax import lax
from jax.experimental import pallas as pl
from jax.experimental.pallas import tpu as pltpu
from jax.sharding import PartitionSpec as P

MIB = 1 << 20
VMEM = pl.BlockSpec(memory_space=pltpu.VMEM)
ANY = pl.BlockSpec(memory_space=pl.ANY)
SMEM = pl.BlockSpec(memory_space=pltpu.SMEM)
BF16, F32 = jnp.bfloat16, jnp.float32


def params(mib):
    return pltpu.CompilerParams(vmem_limit_bytes=mib * MIB)


def sizes_of(half):
    if half % 4 or half < 8:
        return [2] * (half // 2)
    return [2] + [4] * (half // 4 - 1) + [2]


PAD = 16
LANES = 128


def split_decays(decay):
    pieces = []
    rest = decay
    for _ in range(3):
        part = rest.astype(BF16).astype(F32)
        rest = rest - part
        pieces += [part[:, i : i + LANES] for i in range(0, decay.shape[1], LANES)]
    pieces += [jnp.zeros_like(pieces[0])] * (PAD - len(pieces))
    return jnp.concatenate(pieces, axis=0).astype(BF16)


def join_decays(block, count):
    block = block.astype(F32)
    n = count // LANES
    parts = [block[i : i + 1] + block[n + i : n + i + 1] + block[2 * n + i : 2 * n + i + 1] for i in range(n)]
    return jnp.concatenate(parts, axis=1)


def columns(*rows):
    rows = list(rows) + [rows[0]] * (8 - len(rows))
    return jnp.transpose(jnp.concatenate(rows, axis=0))


TOKEN = jax.ShapeDtypeStruct((8, 128), F32)


def call(kernel, out_shape, scalars, operands, after, name, mib=8, scratch=(), specs=None,
         out_specs=None, **more):
    specs = specs or [VMEM] * len(operands)
    out_specs = out_specs or [VMEM] * len(out_shape)
    n, outs = len(scalars) + len(operands), len(out_shape)

    def body(*refs):
        rest = refs[n + len(after) :]
        rest[outs][...] = jnp.zeros(TOKEN.shape, TOKEN.dtype)
        kernel(*refs[:n], *rest[:outs], *rest[outs + 1 :])

    return pl.pallas_call(
        body,
        out_shape=list(out_shape) + [TOKEN],
        in_specs=[SMEM] * len(scalars) + specs + [ANY] * len(after),
        out_specs=list(out_specs) + [VMEM],
        scratch_shapes=list(scratch),
        compiler_params=params(mib),
        cost_estimate=pl.CostEstimate(flops=1, bytes_accessed=1, transcendentals=0),
        name=name,
        **more,
    )(*scalars, *operands, *after)


def conv(rows_in, halos, weight, decays, lower, edge, sizes, start, count, dtype, after, edges=False, pair=None):
    tile_rows, channels, width = rows_in.shape
    states = weight.shape[2]
    half = tile_rows // 2
    mine = sizes[start : start + count]
    before, total = sum(sizes[:start]), sum(mine)
    whole = start + count == len(sizes)
    assert whole == bool(halos)
    out_shape = [jax.ShapeDtypeStruct((n, states, width), dtype) for n in mine]
    if pair:
        out_shape += [jax.ShapeDtypeStruct((n, states, width), dtype) for n in mine]
    if edges:
        out_shape += [jax.ShapeDtypeStruct((channels, width), rows_in.dtype)] * 2
        out_shape[0] = jax.ShapeDtypeStruct((mine[0] * states + PAD, width), dtype)

    def kernel(lower_ref, edge_ref, rows_ref, weight_ref, decays_ref, *refs):
        refs = list(refs)
        above, below = (refs.pop(0), refs.pop(0)) if whole else (None, None)
        other_ref, coefs_ref = (refs.pop(0), refs.pop(0)) if pair else (None, None)
        shifted, outs = refs.pop(), refs
        low = lower_ref[0]
        first_low, first_up = half + before - 1, half - before - total - 1
        first = first_up + low * (first_low - first_up)
        if edges:
            outs[count][...] = rows_ref[0]
            outs[count + 1][...] = rows_ref[tile_rows - 1]
            outs[0][mine[0] * states :] = split_decays(decays_ref[...])
        lane = lax.broadcasted_iota(jnp.int32, (channels, width), 1)

        def shift(n):
            slot = (total + 1 - n) + low * (2 * n - total - 1)
            if whole and n == total + 1:
                value = jnp.where(low == 1, below[...].astype(F32), above[...].astype(F32))
                value = jnp.where(edge_ref[0] == 1, 0.0, value)
            else:
                value = rows_ref[first + slot].astype(F32)
            left = jnp.where(lane == 0, 0.0, pltpu.roll(value, 1, 1))
            right = jnp.where(lane == width - 1, 0.0, pltpu.roll(value, width - 1, 1))
            shifted[slot, :channels] = left.astype(BF16)
            shifted[slot, channels : 2 * channels] = value.astype(BF16)
            shifted[slot, 2 * channels :] = right.astype(BF16)

        decay = decays_ref[...]
        gain = columns(jnp.sqrt(1.0 - decay * decay))[:, 0:1]
        taps = jnp.concatenate([weight_ref[i, j] for i in range(3) for j in range(3)], axis=1)
        for n in range(4):
            shift(n)
        done = 0
        for n, size in enumerate(mine):
            for q in range(0, size, 2):
                at = done + q
                r = (total - 2 - at) + low * (2 * at - total + 2)
                window = jnp.concatenate(
                    [
                        jnp.concatenate([shifted[r + i], shifted[r + i + 1]], axis=1)
                        for i in range(3)
                    ],
                    axis=0,
                )
                drive = gain * jnp.dot(taps, window, preferred_element_type=F32)
                place = (size - 2 - q) + low * (2 * q - size + 2)
                for i in range(2):
                    value = drive[:, i * width : (i + 1) * width].astype(dtype)
                    begin = pl.multiple_of((place + i) * states, states)
                    if pair:
                        flat = len(other_ref.shape) == 2
                        other = other_ref[pl.ds(begin, states) if flat else place + i].astype(F32)
                        outs[0][place + i] = jnp.where(low == 1, other, value)
                        outs[1][place + i] = (
                            coefs_ref[:, 1:2] * value + coefs_ref[:, 2:3] * other
                        )
                    elif len(outs[n].shape) == 2:
                        outs[n][pl.ds(begin, states)] = value
                    else:
                        outs[n][place + i] = value
                for i in range(at + 4, min(at + 6, total + 2)):
                    shift(i)
            done += size

    return call(
        kernel, out_shape, [lower, edge],
        [rows_in, weight, decays] + list(halos) + list(pair or []), after, "conv_chunks", 14,
        scratch=[pltpu.VMEM((total + 2, 3 * channels, width), rows_in.dtype)],
    )


def coefficients(odd, own_decay, first, after):
    def kernel(odd_ref, own_ref, first_ref, out):
        is_odd = jnp.full(own_ref.shape, odd_ref[0], jnp.int32) == 1
        own = own_ref[...]
        other = join_decays(first_ref[first.shape[0] - PAD :], own.shape[1])
        both = own * other
        one = jnp.ones_like(own)
        out[...] = columns(
            both,
            jnp.where(is_odd, one, other),
            jnp.where(is_odd, own, one),
            jnp.where(is_odd, other, own),
        )

    shape = jax.ShapeDtypeStruct((own_decay.shape[1], 8), F32)
    return call(kernel, [shape], [odd], [own_decay, first], after, "coefficients")


def carry_on(group, coefs, drives, carry, after):
    groups = sorted(drives)
    most = max(drives[g].shape[0] for g in groups)
    shape = jax.ShapeDtypeStruct((most,) + drives[groups[0]].shape[1:], BF16)

    def kernel(group_ref, coefs_ref, *refs):
        out = refs[-1]
        for g, ref in zip(groups, refs):

            @pl.when(group_ref[0] == g)
            def one(g=g, ref=ref):
                for q in range(ref.shape[0]):
                    total = ref[q]
                    if g > 0:
                        total = total + coefs_ref[:, 0:1] * refs[len(groups)][q].astype(F32)
                    out[q] = total.astype(BF16)

    operands = [coefs] + [drives[g] for g in groups] + ([carry] if carry is not None else [])
    return call(kernel, [shape], [group], operands, after, "carry_on")


def states_of(group, odd, coefs, first, pair, carries, after):
    shape = jax.ShapeDtypeStruct(first.shape, BF16)

    def kernel(group_ref, odd_ref, coefs_ref, first_ref, pair_ref, *refs):
        own, back = refs[-2:]

        def settle(carry_ref, of_even, of_odd):
            for q in range(first.shape[0]):
                even_state, odd_state = first_ref[q], pair_ref[q]
                if carry_ref is not None:
                    carry = carry_ref[q].astype(F32)
                    even_state = even_state + coefs_ref[:, 3:4] * carry
                    odd_state = odd_state + coefs_ref[:, 0:1] * carry
                of_even[q] = even_state.astype(BF16)
                of_odd[q] = odd_state.astype(BF16)

        for g in range(len(carries) + 1):
            carry_ref = refs[g - 1] if g else None
            here = group_ref[0] == g
            pl.when(here & (odd_ref[0] == 0))(functools.partial(settle, carry_ref, own, back))
            pl.when(here & (odd_ref[0] == 1))(functools.partial(settle, carry_ref, back, own))

    operands = [coefs, first, pair] + list(carries)
    return call(kernel, [shape, shape], [group, odd], operands, after, "states_of")


def output_half(lower, rows_in, weight, skip, states, begun, earlier, after, dtype, finish=True):
    tile_rows, channels, width = rows_in.shape
    half = tile_rows // 2
    pitch = channels + 1
    sizes = sizes_of(half)
    here = [n for n, value in enumerate(states) if value is not None]
    count = len(here)
    blocks = 4 if channels % 64 == 0 else 1
    held_rows = (half + 1) * pitch + 7

    def kernel(lower_ref, rows_ref, weight_ref, skip_ref, *refs):
        chunks = dict(zip(here, refs[:count]))
        if finish:
            total, tile, sems = refs[-3:]
            out = refs[-4]
        else:
            total = refs[-1]
        low = lower_ref[0]
        begin = pl.multiple_of(low * half, half)
        gain = columns(skip_ref[...])[:, 0:1]
        for n, chunk in chunks.items():
            done = sum(sizes[:n])
            at_up = half - done - sizes[n]
            r = at_up + low * (done - at_up)
            for q in range(0, sizes[n], 2):
                value = jnp.dot(
                    weight_ref[...],
                    jnp.concatenate([chunk[q], chunk[q + 1]], axis=1),
                    preferred_element_type=F32,
                )
                for i in range(2):
                    total[pl.ds((r + q + i) * pitch, channels), :] = value[
                        :, i * width : (i + 1) * width
                    ] + gain * rows_ref[begin + r + q + i].astype(F32)
        if not finish:
            return
        if begun is not None:
            begun_ref = refs[count]
            now = [sum(sizes[: here[0]]), sum(sizes[: here[-1] + 1])]
            low_at = [half - now[1], half - now[0]]
            first = low_at[0] + low * (now[0] - low_at[0])
            last_row = low_at[1] + low * (now[1] - low_at[1])
            at = lax.broadcasted_iota(jnp.int32, (half, width), 0)
            fresh = (at >= first) & (at < last_row)

        def settle(n, carry):
            for i in range(8):
                value = total[pl.ds(n * 8 + i, half, stride=pitch), :]
                if begun is not None:
                    old = begun_ref[pl.ds(n * 8 + i, half, stride=pitch), :]
                    value = jnp.where(fresh, value, old)
                tile[n * 8 + i] = value.astype(dtype)
            return carry

        copies = []
        size = channels // blocks
        for n in range(blocks):
            lax.fori_loop(n * size // 8, (n + 1) * size // 8, settle, 0, unroll=4)
            part = pl.ds(n * size, size)
            copies.append(
                pltpu.make_async_copy(
                    tile.at[part], out.at[part, pl.ds(begin, half), :], sems.at[n]
                )
            )
            copies[-1].start()
        for copy in copies:
            copy.wait()

    operands = [rows_in, weight, skip] + [states[n] for n in here]
    if begun is not None:
        operands.append(begun)
    in_place = len(operands)
    more = {}
    if earlier is not None:
        operands.append(earlier)
        more["input_output_aliases"] = {len(operands): 0}
    specs = [VMEM] * in_place + [ANY] * (len(operands) - in_place)
    if not finish:
        shape = jax.ShapeDtypeStruct((held_rows, width), F32)
        return call(kernel, [shape], [lower], operands, after, "output_begun", 10, specs=specs)
    return call(
        kernel,
        [jax.ShapeDtypeStruct((channels, tile_rows, width), dtype)],
        [lower], operands, after, "output_half", 10,
        scratch=[
            pltpu.VMEM((held_rows, width), F32),
            pltpu.VMEM((channels, half, width), dtype),
            pltpu.SemaphoreType.DMA((blocks,)),
        ],
        specs=specs,
        out_specs=[ANY],
        **more,
    )


def on_device(frames_in, conv_weight, out_weight, skip_gain, decays):
    tile_rows = frames_in.shape[2]
    frames = lax.axis_size("tm")
    spaces = lax.axis_size("space")
    groups = frames // 2
    me, at = lax.axis_index("tm"), lax.axis_index("space")
    scalar = lambda value: jnp.asarray(value, jnp.int32).reshape(1)
    group, odd, even = scalar(me // 2), scalar(me % 2), scalar(1 - me % 2)
    is_top, is_bottom = scalar(at == 0), scalar(at == spaces - 1)
    is_even = me % 2 == 0
    sizes = sizes_of(tile_rows // 2)
    chunks = len(sizes)

    swap = [(i, i + 1 - 2 * (i % 2)) for i in range(frames)]
    even_hop = [(i, i + 2 if (i // 2) % 2 == 0 else i - 2) for i in range(frames)]
    odd_hop = [
        (i * spaces + j, i * spaces + j + 1 - 2 * (j % 2))
        if i // 2 in (0, groups - 1)
        else (i * spaces + j, (i + 2 if (i // 2) % 2 else i - 2) * spaces + j)
        for i in range(frames)
        for j in range(spaces)
    ]
    down = [(i, (i + 1) % spaces) for i in range(spaces)]
    up = [(i, (i - 1) % spaces) for i in range(spaces)]

    rows = jnp.transpose(frames_in[0], (1, 0, 2))
    sent = functools.partial(
        conv, rows, weight=conv_weight, decays=decays, lower=even,
        edge=jnp.where(is_even, is_bottom, is_top), sizes=sizes, dtype=BF16,
    )
    kept = functools.partial(
        conv, rows, weight=conv_weight, decays=decays, lower=odd,
        edge=jnp.where(is_even, is_top, is_bottom), sizes=sizes, dtype=F32,
    )
    early = 2
    *mine, top, bottom, token = sent(halos=[], start=0, count=early, after=[], edges=True)
    others = [lax.ppermute(value, "tm", swap) for value in mine]
    halos = [lax.ppermute(bottom, "space", down), lax.ppermute(top, "space", up)]
    coefs, token = coefficients(odd, decays, others[0], [token])
    held, drives = [], []

    def pair_drive(k, token, after=[]):
        keep, drive, token = kept(
            halos=halos if k == chunks - 1 else [], start=k, count=1, after=[token] + after,
            pair=[others[k], coefs],
        )
        held.append(keep)
        drives.append(drive)
        return token

    token = pair_drive(0, token)
    lag = 3 * ((groups - 2) // 2) + 1
    evens, odds, own, back = {}, {}, [], []
    waits = {('O', lag + 1): [0], ('E', lag + 3): [1], ('S', lag + chunks - 1): [chunks - 3]}

    def held_up(kind, step):
        return [back[n] for n in waits.get((kind, step), []) if 0 <= n < len(back)]

    for step in range(chunks + lag):
        ready = {
            g: drives[step - 3 * (g // 2)]
            for g in range(0, groups - 1, 2)
            if 0 <= step - 3 * (g // 2) < chunks
        }
        if ready:
            after = [token] + [] + held_up('E', step)
            value, token = carry_on(group, coefs, ready, odds.get(step - 2), after)
            evens[step] = lax.ppermute(value, "tm", even_hop)
        if step == 0:
            *rest, token = sent(halos=halos, start=early, count=chunks - early, after=[token])
            others += [lax.ppermute(value, "tm", swap) for value in rest]
        k = step - lag
        if k >= 0:
            carries = [
                evens[k + 3 * ((g - 1) // 2)] if g % 2 else odds[k + 1 + 3 * ((g - 2) // 2)]
                for g in range(1, groups)
            ]
            after = [token] + held_up('S', step)
            mine, theirs, token = states_of(group, odd, coefs, held[k], drives[k], carries, after)
            own.append(mine)
            back.append(lax.ppermute(theirs, "tm", swap))
        ready = {
            g: drives[step - 1 - 3 * ((g - 1) // 2)]
            for g in range(1, groups - 1, 2)
            if 0 <= step - 1 - 3 * ((g - 1) // 2) < chunks
        }
        if ready:
            value, token = carry_on(group, coefs, ready, evens[step - 1], [token] + held_up('O', step))
            odds[step] = lax.ppermute(value, ("tm", "space"), odd_hop)
        if step + 1 < chunks:
            token = pair_drive(step + 1, token, [evens[0]] if step == 0 else [])

    skip = skip_gain[None]
    dtype = frames_in.dtype
    half_done, token = output_half(
        odd, rows, out_weight, skip, own, None, None, [token], dtype
    )
    begun, token = output_half(
        even, rows, out_weight, skip, back[:-2] + [None] * 2, None, None, [token], dtype, finish=False
    )
    result, token = output_half(
        even, rows, out_weight, skip, [None] * (chunks - 2) + back[-2:], begun, half_done,
        [token], dtype,
    )
    return result[None]


def solution(mesh):
    placed = (P("tm", None, "space", None), P(), P(), P(), P("tm", None))
    return jax.shard_map(
        on_device,
        mesh=mesh,
        in_specs=placed,
        out_specs=P("tm", None, "space", None),
        check_vma=False,
    )
```
